256 devices in a mesh: row: 16 (over y, x_hi, core), col: 16 (over x_lo, z).
Axes of the slice: x: 4 (x_hi: 2, x_lo: 2; x = x_hi * 2 + x_lo), y: 4, z: 8, core: 2. Of those that a mesh axis runs over, the one named last changes fastest.
Arguments:
- object_field: float32 [2, 4096, 4096], P(None, 'row', 'col'), may hold values from -3 to 4
- probe_modes: float32 [2, 4, 128, 128], replicated, may hold values from -3 to 3
- scan_offsets: int32 [16, 16, 16, 2], P('row', 'col'), may hold values from 0 to 255
- measured: float32 [16, 16, 16, 128, 128], P('row', 'col'), may hold values from 0 to 24
Outputs:
- object_out: float32 [2, 4096, 4096], P(None, 'row', 'col')
- probe_out: float32 [2, 4, 128, 128], replicated
The draws below stay inside these ranges and needn't reach their ends.
All inputs are finite; a program needn't handle non-finite values.
Results may differ from the reference program's by a relative error of at most 0.003.
The reference program's roundings to bfloat16 on the way count: a program that leaves them out, or rounds other values in their place, can miss the bound.
Values sent between devices are 32-bit elements; how exact they have to be, the bound alone decides.
No kernel may reach another device: no remote copies, remote signals or barrier semaphores. Data moves between devices by JAX's collectives and lax.ppermute only.
A program may use at most 64 MiB of HBM per device.

```python
import jax
import jax.numpy as jnp
from jax import lax

PATCH = 128
MODES = 4
TILE = 256
POS_DEV = 16
ITERS = 2
HALF = 64
NY = 4096
NX = 4096
N_ROW = 16
N_COL = 16


def draw_object_field(key, part):
    key = jax.random.fold_in(key, 11)
    real_key, imag_key = jax.random.split(key)
    rough_re = jnp.clip(0.7 * jax.random.normal(real_key, (NY, NX), jnp.float32), -2.8, 2.8)
    rough_im = jnp.clip(0.7 * jax.random.normal(imag_key, (NY, NX), jnp.float32), -2.8, 2.8)
    common = 0.8
    return jnp.stack([rough_re + common, rough_im]).astype(jnp.float32)


def draw_measured(key, part):
    key = jax.random.fold_in(key, 7)
    scale_key, base_key = jax.random.split(key)
    low_log = jnp.log(jnp.float32(0.25))
    high_log = jnp.log(jnp.float32(12.0))
    tile_scale = jnp.exp(jax.random.uniform(scale_key, (N_ROW, N_COL, 1, 1, 1), jnp.float32, low_log, high_log))
    uniform_base = jax.random.uniform(base_key, (N_ROW, N_COL, POS_DEV, PATCH, PATCH), jnp.float32, 0.0, 1.0)
    pixels = jnp.arange(PATCH, dtype=jnp.int32)
    wrapped = jnp.minimum(pixels, PATCH - pixels).astype(jnp.float32) / HALF
    radius_sq = wrapped[:, None] * wrapped[:, None] + wrapped[None, :] * wrapped[None, :]
    envelope = 0.25 + 0.75 * jnp.exp(-radius_sq / 0.2)
    base = 2.0 * uniform_base
    return (base * envelope * tile_scale).astype(jnp.float32)


def set_ends(result, own_key, least, top_value):
    index_at = [jax.random.randint(jax.random.fold_in(own_key, axis), (), 0, length) for axis, length in enumerate(result.shape)]
    main_axis = result.shape.index(max(result.shape))
    neighbour = index_at[:main_axis] + [(index_at[main_axis] + 1) % result.shape[main_axis]] + index_at[main_axis + 1:]
    return result.at[tuple(index_at)].set(least).at[tuple(neighbour)].set(top_value)


def noise(key, shape, deviation, reach, held_as=jnp.bfloat16):
    values = deviation * jax.random.normal(key, shape, jnp.float32)
    return jnp.clip(values, min=-reach, max=reach).astype(held_as)


def setup_inputs(seed: int = 0) -> dict:
    seeds = jax.random.split(jax.random.key(seed), 5)
    return {
        "object_field": draw_object_field(jax.random.fold_in(seeds[4], 71), 0),
        "probe_modes": noise(seeds[1], (2, MODES, PATCH, PATCH), 0.5, 3.0, jnp.float32),
        "scan_offsets": set_ends(jax.random.randint(seeds[2], (N_ROW, N_COL, POS_DEV, 2), 0, TILE), jax.random.fold_in(seeds[2], 1), 0, TILE - 1).astype(jnp.int32),
        "measured": draw_measured(jax.random.fold_in(seeds[4], 71), 0),
    }


def dft_tables(patch_len, inverse):
    indices = jnp.arange(patch_len, dtype=jnp.int32)
    phases = indices[:, None] * indices[None, :] % patch_len
    radians = phases.astype(jnp.float32) * (2.0 * jnp.pi / patch_len)
    factor = 1.0 / jnp.sqrt(jnp.float32(patch_len))
    cosine = jnp.cos(radians) * factor
    sine_part = jnp.sin(radians) * factor
    imag_part = sine_part if inverse else -sine_part
    left_table = jnp.concatenate([jnp.concatenate([cosine, -imag_part], 1), jnp.concatenate([imag_part, cosine], 1)], 0)
    right_table = jnp.concatenate([cosine, imag_part], 1)
    return (left_table.astype(jnp.bfloat16), right_table.astype(jnp.bfloat16))

def transform(field_low, tables, patch_len):
    field_in = lax.optimization_barrier(field_low).astype(jnp.float32)
    stacked = field_in.reshape(field_in.shape[:-3] + (2 * patch_len, patch_len))
    sectioned = jnp.einsum('ij,bmjk->bmik', tables[0].astype(jnp.float32), stacked).astype(jnp.bfloat16)
    sectioned = lax.optimization_barrier(sectioned).astype(jnp.float32)
    product = jnp.einsum('bmij,jk->bmik', sectioned, tables[1].astype(jnp.float32))
    upper_half = product[:, :, :patch_len, :]
    lower_half = product[:, :, patch_len:, :]
    real_out = upper_half[..., :patch_len] - lower_half[..., patch_len:]
    imag_out = upper_half[..., patch_len:] + lower_half[..., :patch_len]
    return (real_out, imag_out)

def wave_terms(windows, probes, amplitude, forward, backward, patch_len):
    probe_re = probes[0][None]
    probe_im = probes[1][None]
    window_re = windows[:, 0][:, None]
    window_im = windows[:, 1][:, None]
    exit_re = probe_re * window_re - probe_im * window_im
    exit_im = probe_re * window_im + probe_im * window_re
    exit_wave = jnp.stack([exit_re, exit_im], axis=2).astype(jnp.bfloat16)
    far_re, far_im = transform(exit_wave, forward, patch_len)
    intensity = lax.optimization_barrier(jnp.sum(far_re * far_re + far_im * far_im, axis=1))
    scaling = (amplitude / jnp.sqrt(intensity + 1.0))[:, None]
    corrected = jnp.stack([far_re * scaling, far_im * scaling], axis=2).astype(jnp.bfloat16)
    back_re, back_im = transform(corrected, backward, patch_len)
    diff_re = back_re - exit_re
    diff_im = back_im - exit_im
    object_re = lax.optimization_barrier(jnp.sum(probe_re * diff_re + probe_im * diff_im, axis=1))
    object_im = lax.optimization_barrier(jnp.sum(probe_re * diff_im - probe_im * diff_re, axis=1))
    grad_re = lax.optimization_barrier(jnp.sum(window_re * diff_re + window_im * diff_im, axis=0))
    grad_im = lax.optimization_barrier(jnp.sum(window_re * diff_im - window_im * diff_re, axis=0))
    density = lax.optimization_barrier(jnp.sum(windows[:, 0] * windows[:, 0] + windows[:, 1] * windows[:, 1], axis=0))
    return (object_re, object_im, jnp.stack([grad_re, grad_im]), density)

def reference(object_field, probe_modes, scan_offsets, measured):
    half_len = PATCH // 2
    forward = dft_tables(PATCH, False)
    backward = dft_tables(PATCH, True)
    tile_rows = jnp.arange(N_ROW, dtype=jnp.int32)[:, None, None] * TILE
    tile_cols = jnp.arange(N_COL, dtype=jnp.int32)[None, :, None] * TILE
    row_starts = (scan_offsets[..., 0] + tile_rows).astype(jnp.int32).reshape(N_ROW * N_COL, POS_DEV)
    col_starts = (scan_offsets[..., 1] + tile_cols).astype(jnp.int32).reshape(N_ROW * N_COL, POS_DEV)
    amplitudes = measured.reshape(N_ROW * N_COL, POS_DEV, PATCH, PATCH)
    zero_index = jnp.zeros((), jnp.int32)
    current = object_field
    probes = probe_modes
    for sweep in range(ITERS):
        padded = jnp.pad(current, ((0, 0), (half_len, half_len), (half_len, half_len)))
        lighting = lax.optimization_barrier(jnp.sum(probes[0] * probes[0] + probes[1] * probes[1], axis=0))

        def cut_window(row_start, col_start):
            return lax.dynamic_slice(padded, (zero_index, row_start, col_start), (2, PATCH, PATCH))

        def visit(running, element):
            placed, probe_grad, density = running
            row_group, col_group, amplitude = element
            windows = jax.vmap(cut_window)(row_group, col_group)
            object_re, object_im, grad_part, density_part = wave_terms(windows, probes, amplitude, forward, backward, PATCH)

            def place(slot, canvas):
                start = (zero_index, row_group[slot], col_group[slot])
                contrib = jnp.stack([object_re[slot], object_im[slot], lighting])
                region = lax.dynamic_slice(canvas, start, (3, PATCH, PATCH))
                return lax.dynamic_update_slice(canvas, region + contrib, start)
            placed = lax.fori_loop(0, POS_DEV, place, placed)
            return ((placed, probe_grad + grad_part, density + density_part), None)
        initial = (jnp.zeros((3, NY + PATCH, NX + PATCH), jnp.float32), jnp.zeros((2, MODES, PATCH, PATCH), jnp.float32), jnp.zeros((PATCH, PATCH), jnp.float32))
        summed, _ = lax.scan(visit, initial, (row_starts, col_starts, amplitudes))
        placed, probe_grad, density = summed
        interior = placed[:, half_len:half_len + NY, half_len:half_len + NX]
        light_max = jnp.max(interior[2])
        current = current + interior[:2] / (interior[2] + 0.1 * light_max)
        probes = probes + probe_grad / (density + 0.1 * jnp.max(density))
    return (current, probes)
```

```python
import functools

import jax
import jax.numpy as jnp
import numpy as np
from jax import lax
from jax.experimental import pallas as pl
from jax.experimental.pallas import tpu as pltpu
from jax.sharding import PartitionSpec as P

ITERS = 2
BATCH = 2


def dft_pair(n):
    index = np.arange(n)
    angle = (index[:, None] * index[None, :] % n) * (2.0 * np.pi / n)
    c = np.cos(angle) / np.sqrt(n)
    s = np.sin(angle) / np.sqrt(n)
    forward = np.block([[c, s], [-s, c]])
    backward = np.block([[c, -s], [s, c]])
    return jnp.asarray(forward, jnp.bfloat16), jnp.asarray(backward, jnp.bfloat16)


def spot(off_ref, q, n):
    u = off_ref[q, 0]
    v = off_ref[q, 1]
    return u, v // n, lax.rem(v, n)


def place(canvas, ch, where, lane, value):
    u, k, s = where
    n = value.shape[0]
    rolled = pltpu.roll(value, s, 1)
    canvas[ch, k, pl.ds(u, n), :] += jnp.where(lane >= s, rolled, 0.0)
    canvas[ch, k + 1, pl.ds(u, n), :] += jnp.where(lane >= s, 0.0, rolled)


def light_kernel(off_ref, probe_ref, placed_ref, canvas):
    n = probe_ref.shape[2]
    lane = lax.broadcasted_iota(jnp.int32, (n, n), 1)
    light = jnp.sum(probe_ref[0] * probe_ref[0] + probe_ref[1] * probe_ref[1], axis=0)
    canvas[...] = jnp.zeros_like(canvas)

    def step(q, carry):
        place(canvas, 0, spot(off_ref, q, n), lane, light)
        return carry

    lax.fori_loop(0, off_ref.shape[0], step, 0)
    for k in range(canvas.shape[1]):
        placed_ref[:, k * n : (k + 1) * n] = canvas[0, k]


def sweep_kernel(
    off_ref, obj_ref, probe_ref, meas_ref, fwd_ref, bwd_ref, placed_ref, grad_ref, cells, canvas
):
    modes = probe_ref.shape[1]
    n = probe_ref.shape[2]
    blocks = cells.shape[1]
    for k in range(blocks):
        cells[:, k] = obj_ref[:, :, k * n : (k + 1) * n]
    canvas[...] = jnp.zeros_like(canvas)
    grad_ref[...] = jnp.zeros_like(grad_ref)
    lane = lax.broadcasted_iota(jnp.int32, (n, n), 1)

    def window(ch, where):
        u, k, s = where
        left = cells[ch, k, pl.ds(u, n), :]
        right = cells[ch, k + 1, pl.ds(u, n), :]
        return pltpu.roll(jnp.where(lane >= s, left, right), n - s, 1)

    def transform(field, left, right):
        sec = jnp.dot(left, field, preferred_element_type=jnp.float32).astype(jnp.bfloat16)
        parts = [slice(m * n, (m + 1) * n) for m in range(modes)]
        rows = [jnp.concatenate([sec[:n, part], sec[n:, part]], 1) for part in parts]
        return jnp.dot(jnp.concatenate(rows, 0), right, preferred_element_type=jnp.float32)

    def paired(re_parts, im_parts):
        re_all = jnp.concatenate([x.astype(jnp.bfloat16) for x in re_parts], 1)
        im_all = jnp.concatenate([x.astype(jnp.bfloat16) for x in im_parts], 1)
        return jnp.concatenate([re_all, im_all], 0)

    def split(wave):
        return [(wave[m * n : (m + 1) * n, :n], wave[m * n : (m + 1) * n, n:]) for m in range(modes)]

    def step(i, carry):
        probes = [(probe_ref[0, m], probe_ref[1, m]) for m in range(modes)]
        spots = [spot(off_ref, i * BATCH + j, n) for j in range(BATCH)]
        wins = [(window(0, where), window(1, where)) for where in spots]
        exits = []
        for w_re, w_im in wins:
            re_parts = [p_re * w_re - p_im * w_im for p_re, p_im in probes]
            im_parts = [p_re * w_im + p_im * w_re for p_re, p_im in probes]
            exits.append(paired(re_parts, im_parts))
        fars = [split(transform(x, fwd_ref[...], bwd_ref[...])) for x in exits]
        corrected = []
        for j, far in enumerate(fars):
            power = functools.reduce(jnp.add, [re * re + im * im for re, im in far])
            scale = meas_ref[i * BATCH + j] / jnp.sqrt(power + 1.0)
            corrected.append(paired([re * scale for re, _ in far], [im * scale for _, im in far]))
        backs = [split(transform(x, bwd_ref[...], fwd_ref[...])) for x in corrected]
        for where, back in zip(spots, backs):
            terms_re = [p[0] * b[0] + p[1] * b[1] for p, b in zip(probes, back)]
            terms_im = [p[0] * b[1] - p[1] * b[0] for p, b in zip(probes, back)]
            place(canvas, 0, where, lane, functools.reduce(jnp.add, terms_re))
            place(canvas, 1, where, lane, functools.reduce(jnp.add, terms_im))
        for m in range(modes):
            pairs = [(w, back[m]) for w, back in zip(wins, backs)]
            grad_ref[m] += functools.reduce(jnp.add, [w[0] * b[0] + w[1] * b[1] for w, b in pairs])
            grad_ref[modes + m] += functools.reduce(
                jnp.add, [w[0] * b[1] - w[1] * b[0] for w, b in pairs]
            )
        grad_ref[2 * modes] += functools.reduce(jnp.add, [w[0] * w[0] + w[1] * w[1] for w in wins])
        return carry

    lax.fori_loop(0, meas_ref.shape[0] // BATCH, step, 0)
    for k in range(blocks):
        placed_ref[:, :, k * n : (k + 1) * n] = canvas[:, k]


VM = pl.BlockSpec(memory_space=pltpu.VMEM)
SM = pl.BlockSpec(memory_space=pltpu.SMEM)


def place_light(offsets, probes, extent):
    n = probes.shape[-1]
    return pl.pallas_call(
        light_kernel,
        out_shape=jax.ShapeDtypeStruct((extent, extent), jnp.float32),
        in_specs=[SM, VM],
        out_specs=VM,
        scratch_shapes=[pltpu.VMEM((1, extent // n, extent, n), jnp.float32)],
        compiler_params=pltpu.CompilerParams(vmem_limit_bytes=16 * 1024 * 1024),
        name="place_light",
    )(offsets, probes)


def sweep_tile(offsets, padded, probes, measured, tables):
    n = probes.shape[-1]
    extent = padded.shape[1]
    shape = (2, extent // n, extent, n)
    return pl.pallas_call(
        sweep_kernel,
        out_shape=(
            jax.ShapeDtypeStruct(padded.shape, jnp.float32),
            jax.ShapeDtypeStruct((2 * probes.shape[1] + 1, n, n), jnp.float32),
        ),
        in_specs=[SM] + [VM] * 5,
        out_specs=(VM, VM),
        scratch_shapes=[pltpu.VMEM(shape, jnp.float32)] * 2,
        compiler_params=pltpu.CompilerParams(vmem_limit_bytes=48 * 1024 * 1024),
        name="sweep_tile",
    )(offsets, padded, probes, measured, *tables)


def shift_up(axis):
    count = lax.axis_size(axis)
    return [(i, i + 1) for i in range(count - 1)]


def shift_down(axis):
    count = lax.axis_size(axis)
    return [(i + 1, i) for i in range(count - 1)]


def pad_tile(cells, width):
    for axis, dim in (("row", 1), ("col", 2)):
        size = cells.shape[dim]
        head = lax.slice_in_dim(cells, 0, width, axis=dim)
        tail = lax.slice_in_dim(cells, size - width, size, axis=dim)
        before = lax.ppermute(tail, axis, shift_up(axis))
        after = lax.ppermute(head, axis, shift_down(axis))
        cells = jnp.concatenate([before, cells, after], axis=dim)
    return cells


def sum_overlaps(cells, band):
    for axis, dim in (("row", 1), ("col", 2)):
        size = cells.shape[dim]
        head = lax.slice_in_dim(cells, 0, band, axis=dim)
        middle = lax.slice_in_dim(cells, band, size - band, axis=dim)
        tail = lax.slice_in_dim(cells, size - band, size, axis=dim)
        head = head + lax.ppermute(tail, axis, shift_up(axis))
        tail = tail + lax.ppermute(
            lax.slice_in_dim(cells, 0, band, axis=dim), axis, shift_down(axis)
        )
        cells = jnp.concatenate([head, middle, tail], axis=dim)
    return cells


def body(object_field, probe_modes, scan_offsets, measured):
    n = probe_modes.shape[-1]
    modes = probe_modes.shape[1]
    half = n // 2
    tile = object_field.shape[1]
    extent = tile + n
    positions = scan_offsets.shape[2]
    offsets = scan_offsets.reshape(positions, 2)
    amplitudes = measured.reshape(positions, n, n)
    tables = dft_pair(n)
    inside = np.ones((extent, extent), bool)
    for axis, dim in (("row", 0), ("col", 1)):
        at = lax.broadcasted_iota(jnp.int32, (extent, extent), dim)
        at = at + lax.axis_index(axis) * tile - half
        inside = inside & (at >= 0) & (at < tile * lax.axis_size(axis))
    probes = probe_modes
    padded = pad_tile(object_field, half)
    for sweep in range(ITERS):
        light = place_light(offsets, probes, extent)
        light = sum_overlaps(light[None], n)[0]
        light_max = lax.pmax(jnp.max(light[half : half + tile, half : half + tile]), ("row", "col"))
        placed, grads = sweep_tile(offsets, padded, probes, amplitudes, tables)
        placed = sum_overlaps(placed, n)
        step = (placed - padded * light) / (light + 0.1 * light_max)
        padded = jnp.where(inside, padded + step, 0.0)
        totals = lax.psum(grads, ("row", "col"))
        density = totals[2 * modes]
        sums = totals[: 2 * modes].reshape(probes.shape)
        probes = probes + (sums - probes * density) / (density + 0.1 * jnp.max(density))
    return padded[:, half : half + tile, half : half + tile], probes


def solution(mesh):
    return jax.shard_map(
        body,
        mesh=mesh,
        in_specs=(
            P(None, "row", "col"),
            P(),
            P("row", "col", None, None),
            P("row", "col", None, None, None),
        ),
        out_specs=(P(None, "row", "col"), P()),
        check_vma=False,
    )
```

```python
import functools

import jax
import jax.numpy as jnp
import numpy as np
from jax import lax
from jax.experimental import pallas as pl
from jax.experimental.pallas import tpu as pltpu
from jax.sharding import Mesh, PartitionSpec as P

ITERS = 2
BATCH = 2
SPLIT = (("y", 4), ("xh", 2), ("core", 2), ("xl", 2), ("z", 8))
ROW = ("y", "xh", "core")
COL = ("xl", "z")
RING = ("y", "z")
PARTS = 32
CHUNK = 24
DATA = 18

VM = pl.BlockSpec(memory_space=pltpu.VMEM)
SM = pl.BlockSpec(memory_space=pltpu.SMEM)
F32 = jnp.float32
SPOTS = pltpu.SMEM((9 * 16 + 1, 2), jnp.int32)


def dft_pair(n):
    index = np.arange(n)
    angle = (index[:, None] * index[None, :] % n) * (2.0 * np.pi / n)
    c = np.cos(angle) / np.sqrt(n)
    s = np.sin(angle) / np.sqrt(n)
    forward = np.block([[c, s], [-s, c]])
    backward = np.block([[c, -s], [s, c]])
    return jnp.asarray(forward, jnp.bfloat16), jnp.asarray(backward, jnp.bfloat16)


def total(values):
    return functools.reduce(jnp.add, values)


def place(canvas, ch, where, lane, value):
    u, k, s = where
    n = value.shape[0]
    rolled = pltpu.roll(value, s, 1)
    canvas[ch, k, pl.ds(u, n), :] += jnp.where(lane >= s, rolled, 0.0)
    canvas[ch, k + 1, pl.ds(u, n), :] += jnp.where(lane >= s, 0.0, rolled)


def sweep_positions(off_ref, probe_ref, meas_ref, fwd_ref, bwd_ref, cells, canvas, grads):
    modes = probe_ref.shape[1]
    n = probe_ref.shape[2]
    canvas[...] = jnp.zeros_like(canvas)
    grads[...] = jnp.zeros_like(grads)
    lane = lax.broadcasted_iota(jnp.int32, (n, n), 1)

    def window(ch, where):
        u, k, s = where
        left = cells[ch, k, pl.ds(u, n), :]
        right = cells[ch, k + 1, pl.ds(u, n), :]
        return pltpu.roll(jnp.where(lane >= s, left, right), n - s, 1)

    def transform(field, left, right):
        sec = jnp.dot(left, field, preferred_element_type=F32).astype(jnp.bfloat16)
        parts = [slice(m * n, (m + 1) * n) for m in range(modes)]
        rows = [jnp.concatenate([sec[:n, part], sec[n:, part]], 1) for part in parts]
        return jnp.dot(jnp.concatenate(rows, 0), right, preferred_element_type=F32)

    def paired(re_parts, im_parts):
        re_all = jnp.concatenate([x.astype(jnp.bfloat16) for x in re_parts], 1)
        im_all = jnp.concatenate([x.astype(jnp.bfloat16) for x in im_parts], 1)
        return jnp.concatenate([re_all, im_all], 0)

    def split(wave):
        return [(wave[m * n : (m + 1) * n, :n], wave[m * n : (m + 1) * n, n:]) for m in range(modes)]

    def spot(q):
        u = off_ref[q, 0]
        v = off_ref[q, 1]
        return u, v // n, lax.rem(v, n)

    def step(i, carry):
        probes = [(probe_ref[0, m], probe_ref[1, m]) for m in range(modes)]
        spots = [spot(i * BATCH + j) for j in range(BATCH)]
        wins = [(window(0, where), window(1, where)) for where in spots]
        exits = []
        for w_re, w_im in wins:
            re_parts = [p_re * w_re - p_im * w_im for p_re, p_im in probes]
            im_parts = [p_re * w_im + p_im * w_re for p_re, p_im in probes]
            exits.append(paired(re_parts, im_parts))
        fars = [split(transform(x, fwd_ref[...], bwd_ref[...])) for x in exits]
        corrected = []
        for j, far in enumerate(fars):
            power = total([re * re + im * im for re, im in far])
            scale = meas_ref[i * BATCH + j] / jnp.sqrt(power + 1.0)
            corrected.append(paired([re * scale for re, _ in far], [im * scale for _, im in far]))
        backs = [split(transform(x, bwd_ref[...], fwd_ref[...])) for x in corrected]
        for where, back in zip(spots, backs):
            place(canvas, 0, where, lane, total([p[0] * b[0] + p[1] * b[1] for p, b in zip(probes, back)]))
            place(canvas, 1, where, lane, total([p[0] * b[1] - p[1] * b[0] for p, b in zip(probes, back)]))
        for m in range(modes):
            pairs = [(w, back[m]) for w, back in zip(wins, backs)]
            grads[m] += total([w[0] * b[0] + w[1] * b[1] for w, b in pairs])
            grads[modes + m] += total([w[0] * b[1] - w[1] * b[0] for w, b in pairs])
        grads[2 * modes] += total([w[0] * w[0] + w[1] * w[1] for w in wins])
        return carry

    lax.fori_loop(0, meas_ref.shape[0] // BATCH, step, 0)


def pack_half(grads, half, out_ref):
    planes = grads.shape[0]
    out_ref[...] = jnp.zeros_like(out_ref)
    for c in range(planes):
        for t in range(2):
            out_ref[pl.ds(2 * c + t, PARTS, stride=CHUNK), :] = grads[
                c, pl.ds(half * 2 * PARTS + t, PARTS, stride=2), :
            ]


def unpack_half(in_ref, half, grads):
    planes = grads.shape[0]
    for c in range(planes):
        for t in range(2):
            grads[c, pl.ds(half * 2 * PARTS + t, PARTS, stride=2), :] = in_ref[
                pl.ds(2 * c + t, PARTS, stride=CHUNK), :
            ]


def finish(copies, at_ref, canvas, grads, top_ref, mid_ref, low_ref, keep_ref, send_ref):
    n = grads.shape[1]
    starts = (0, top_ref.shape[1], top_ref.shape[1] + mid_ref.shape[1])
    for ref, start in zip((top_ref, mid_ref, low_ref), starts):
        for k in range(canvas.shape[1]):
            ref[:, :, k * n : (k + 1) * n] = canvas[:, k, start : start + ref.shape[1]]
        copies.ready(ref)
    for core in range(2):

        @pl.when(at_ref[0] == core)
        def _():
            pack_half(grads, core, keep_ref)
            pack_half(grads, 1 - core, send_ref)


def join_rows_kernel(copies, obj_ref, upper_ref, lower_ref, tag_ref, tall_ref, left_ref, right_ref):
    band = upper_ref.shape[1] - 8
    size = obj_ref.shape[1]
    n = left_ref.shape[1]
    extent = tall_ref.shape[1]
    tall_ref[:, :band] = upper_ref[:, :band]
    copies.need(obj_ref)
    tall_ref[:, band : band + size] = obj_ref[...]
    tall_ref[:, band + size :] = lower_ref[:, :band]
    lane = lax.broadcasted_iota(jnp.int32, (extent, n), 1)
    left_ref[:extent] = jnp.where(lane < band, tall_ref[0, :, :n], pltpu.roll(tall_ref[1, :, :n], band, 1))
    right_ref[:extent] = jnp.where(
        lane < band, pltpu.roll(tall_ref[0, :, size - n :], band, 1), tall_ref[1, :, size - n :]
    )
    for ref in (left_ref, right_ref):
        ref[extent : extent + 1] = upper_ref[0, band : band + 1, :n]
        ref[extent + 1 : extent + 2] = tag_ref[:1]
        ref[extent + 2 : extent + 3] = lower_ref[0, band : band + 1, :n]
        ref[extent + 3 :] = jnp.zeros((5, n), F32)


def first_kernel(
    copies, off_ref, at_ref, tall_ref, before_ref, after_ref, probe_ref, meas_ref, fwd_ref, bwd_ref,
    top_ref, mid_ref, low_ref, keep_ref, send_ref, cells, canvas, grads,
):
    n = probe_ref.shape[2]
    half = n // 2
    extent = tall_ref.shape[1]
    lane = lax.broadcasted_iota(jnp.int32, (extent, n), 1)
    before = before_ref[:extent]
    after = after_ref[:extent]
    strips = [
        (before, pltpu.roll(after, half, 1)),
        (pltpu.roll(before, half, 1), after),
    ]
    for ch in range(2):
        inner = [pltpu.roll(tall_ref[ch, :, k * n : (k + 1) * n], half, 1) for k in range(2)]
        row = [strips[ch][0], *inner, strips[ch][1]]
        for k in range(3):
            cells[ch, k] = jnp.where(lane < half, row[k], row[k + 1])
    copies.ready(cells)
    copies.need(meas_ref, fwd_ref, bwd_ref)
    sweep_positions(off_ref, probe_ref, meas_ref, fwd_ref, bwd_ref, cells, canvas, grads)
    finish(copies, at_ref, canvas, grads, top_ref, mid_ref, low_ref, keep_ref, send_ref)


def light_peak(mine_ref, other_ref):
    best = [jnp.max(ref[pl.ds(DATA, PARTS, stride=CHUNK), :]) for ref in (mine_ref, other_ref)]
    return jnp.maximum(best[0], best[1])


def update_probes(at_ref, mine_ref, other_ref, probe_ref, grads, new_probe_ref):
    modes = probe_ref.shape[1]
    for core in range(2):

        @pl.when(at_ref[0] == core)
        def _():
            unpack_half(mine_ref, core, grads)
            unpack_half(other_ref, 1 - core, grads)

    density = grads[2 * modes]
    scale = 1.0 / (density + 0.1 * jnp.max(density))
    for part in range(2):
        for m in range(modes):
            old = probe_ref[part, m]
            new_probe_ref[part, m] = old + (grads[part * modes + m] - old * density) * scale


def updated(old, sums, light, peak):
    scale = 1.0 / (light + 0.1 * peak)
    return [old[ch] + (sums[ch] - old[ch] * light) * scale for ch in range(2)]


def next_kernel(
    copies, off_ref, at_ref, obj_ref, top_ref, mid_ref, low_ref, left_ref, right_ref, light_ref,
    mine_ref, other_ref, probe_ref, meas_ref, fwd_ref, bwd_ref,
    new_top_ref, new_mid_ref, new_low_ref, keep_ref, send_ref, new_obj_ref, new_probe_ref,
    canvas, grads,
):
    n = probe_ref.shape[2]
    blocks = obj_ref.shape[1]
    copies.need(obj_ref, top_ref, mid_ref, low_ref, left_ref, right_ref, light_ref)
    peak = light_peak(mine_ref, other_ref)
    for j, ref in enumerate((top_ref, mid_ref, low_ref)):
        rows = slice(j * n, (j + 1) * n)
        row = lax.broadcasted_iota(jnp.int32, (n, n), 0) + j * n
        row_ok = (row >= at_ref[1]) & (row < at_ref[2])
        for k in range(blocks):
            col = lax.broadcasted_iota(jnp.int32, (n, n), 1) + k * n
            inside = row_ok & (col >= at_ref[3]) & (col < at_ref[4])
            sums = ref[:, :, k * n : (k + 1) * n]
            if k == 0:
                sums = sums + left_ref[:, rows]
            elif k == blocks - 1:
                sums = sums + right_ref[:, rows]
            new = updated(obj_ref[:, k, rows], sums, light_ref[0, k + 1, n + j * n : 2 * n + j * n], peak)
            for ch in range(2):
                new_obj_ref[ch, k, rows] = jnp.where(inside, new[ch], 0.0)
    copies.ready(new_obj_ref)
    copies.need(probe_ref)
    update_probes(at_ref, mine_ref, other_ref, probe_ref, grads, new_probe_ref)
    copies.ready(new_probe_ref)
    copies.need(meas_ref, fwd_ref, bwd_ref)
    sweep_positions(off_ref, new_probe_ref, meas_ref, fwd_ref, bwd_ref, new_obj_ref, canvas, grads)
    finish(copies, at_ref, canvas, grads, new_top_ref, new_mid_ref, new_low_ref, keep_ref, send_ref)


def last_kernel(
    copies, at_ref, obj_ref, sums_ref, left_ref, right_ref, light_ref, mine_ref, other_ref, probe_ref,
    out_ref, new_probe_ref, grads,
):
    n = probe_ref.shape[2]
    half = n // 2
    blocks = obj_ref.shape[1]
    tile = out_ref.shape[1]
    inner = slice(half, half + tile)
    copies.need(probe_ref)
    update_probes(at_ref, mine_ref, other_ref, probe_ref, grads, new_probe_ref)
    copies.need(obj_ref, sums_ref, left_ref, right_ref, light_ref)
    peak = light_peak(mine_ref, other_ref)
    lane = lax.broadcasted_iota(jnp.int32, (tile, n), 1)
    rolled = []
    for k in range(blocks):
        sums = [sums_ref[ch, :, k * n : (k + 1) * n] for ch in range(2)]
        if k == 0:
            sums[0] = sums[0] + jnp.where(lane < half, 0.0, left_ref[...])
            sums[1] = sums[1] + jnp.where(lane < half, 0.0, pltpu.roll(left_ref[...], half, 1))
        elif k == blocks - 1:
            sums[0] = sums[0] + jnp.where(lane < half, right_ref[...], 0.0)
            sums[1] = sums[1] + jnp.where(lane < half, pltpu.roll(right_ref[...], half, 1), 0.0)
        new = updated(obj_ref[:, k, inner], sums, light_ref[0, k + 1, n + half : n + half + tile], peak)
        rolled.append([pltpu.roll(x, half, 1) for x in new])
    for k in range(blocks - 1):
        for ch in range(2):
            out_ref[ch, :, k * n : (k + 1) * n] = jnp.where(lane < half, rolled[k][ch], rolled[k + 1][ch])


def fold_kernel(copies, top_ref, low_ref, mid_ref, upper_ref, lower_ref, new_top_ref, new_low_ref, left_ref, right_ref):
    n = left_ref.shape[2]
    extent = left_ref.shape[1]
    copies.need(top_ref, low_ref, upper_ref, lower_ref)
    new_top_ref[...] = top_ref[...] + upper_ref[...]
    copies.ready(new_top_ref)
    new_low_ref[...] = low_ref[...] + lower_ref[...]
    copies.ready(new_low_ref)
    copies.need(mid_ref)
    for j, ref in enumerate((new_top_ref, mid_ref, new_low_ref)):
        left_ref[:, j * n : (j + 1) * n] = ref[:, :, :n]
        right_ref[:, j * n : (j + 1) * n] = ref[:, :, extent - n :]
    copies.ready(left_ref, right_ref)


def fold_inner_kernel(copies, mid_ref, upper_ref, lower_ref, sums_ref, left_ref, right_ref):
    n = left_ref.shape[1]
    band = upper_ref.shape[1]
    tile = mid_ref.shape[1]
    extent = mid_ref.shape[2]
    copies.need(mid_ref, upper_ref, lower_ref)
    sums_ref[:, :band] = mid_ref[:, :band] + upper_ref[...]
    sums_ref[:, band : tile - band] = mid_ref[:, band : tile - band]
    sums_ref[:, tile - band :] = mid_ref[:, tile - band :] + lower_ref[...]
    lane = lax.broadcasted_iota(jnp.int32, (tile, n), 1)
    left_ref[...] = jnp.where(lane < band, sums_ref[0, :, :n], pltpu.roll(sums_ref[1, :, :n], band, 1))
    right_ref[...] = jnp.where(
        lane < band, pltpu.roll(sums_ref[1, :, extent - n :], band, 1), sums_ref[0, :, extent - n :]
    )
    copies.ready(sums_ref, left_ref, right_ref)


def place_lights(tag_ref, probe_ref, canvas, spots, rim, tile):
    n = probe_ref.shape[2]
    half = n // 2
    lane = lax.broadcasted_iota(jnp.int32, (n, n), 1)
    value = jnp.sum(probe_ref[0] * probe_ref[0] + probe_ref[1] * probe_ref[1], axis=0)
    count = jnp.int32(0)
    for t in range(9):
        if rim and t == 4:
            continue
        down, across = t % 3 - 1, t // 3 - 1

        def gather(p, count):
            u = tag_ref[t, 2 * p].astype(jnp.int32)
            v = tag_ref[t, 2 * p + 1].astype(jnp.int32)
            held = u > 0
            u = u + (n - 1 + down * tile)
            v = v + (n - 1 + across * tile)
            inner = (u > half) & (u < tile + n + half) & (v > half) & (v < tile + n + half)
            if rim:
                held = held & ~inner & (u > 0) & (u < tile + 2 * n) & (v > 0) & (v < tile + 2 * n)
            else:
                held = held & inner
            spots[count, 0] = u
            spots[count, 1] = v
            return count + held.astype(jnp.int32)

        count = lax.fori_loop(0, tag_ref.shape[1] // 2, gather, count, unroll=4)

    def step(q, carry):
        v = spots[q, 1]
        place(canvas, 0, (spots[q, 0], v // n, lax.rem(v, n)), lane, value)
        return carry

    lax.fori_loop(0, count, step, 0)


def light_kernel(copies, tag_ref, probe_ref, light_ref, peak_ref, spots):
    n = probe_ref.shape[2]
    tile = light_ref.shape[2] - 3 * n
    edge = 3 * n // 2
    blocks = light_ref.shape[1]
    light_ref[...] = jnp.zeros_like(light_ref)
    copies.need(probe_ref)
    place_lights(tag_ref, probe_ref, light_ref, spots, False, tile)
    copies.ready(light_ref)
    lane = lax.broadcasted_iota(jnp.int32, (tile, n), 1)
    best = None
    for k in range(1, blocks - 1):
        mine = light_ref[0, k, edge : edge + tile]
        if k == 1:
            mine = jnp.where(lane >= n // 2, mine, 0.0)
        elif k == blocks - 2:
            mine = jnp.where(lane < n // 2, mine, 0.0)
        best = mine if best is None else jnp.maximum(best, mine)
    peak_ref[...] = jnp.full(peak_ref.shape, jnp.max(best), F32)


def more_light_kernel(copies, tag_ref, probe_ref, light_ref, all_ref, spots):
    copies.need(light_ref, probe_ref)
    all_ref[...] = light_ref[...]
    place_lights(tag_ref, probe_ref, all_ref, spots, True, light_ref.shape[2] - 3 * probe_ref.shape[2])
    copies.ready(all_ref)


def share_kernel(copies, parts_ref, peak_ref, out_ref):
    share = parts_ref[:CHUNK]
    for s in range(1, PARTS):
        share = share + parts_ref[s * CHUNK : (s + 1) * CHUNK]
    row = lax.broadcasted_iota(jnp.int32, share.shape, 0)
    out_ref[...] = jnp.where(row < DATA, share, peak_ref[:1])


class Far:
    def __init__(self, value):
        self.value = value


class Copies:
    def __init__(self, ins, outs):
        self.ins = ins
        self.outs = outs
        for copy in ins.values():
            copy.start()

    def need(self, *refs):
        for ref in refs:
            copy = self.ins.pop(id(ref), None)
            if copy is not None:
                copy.wait()

    def ready(self, *refs):
        for ref in refs:
            copy = self.outs.get(id(ref))
            if copy is not None:
                copy.start()


def call(kernel, outs, scratch, args, scalars, name, limit=24):
    far_in = [isinstance(x, Far) for x in args]
    far_out = [isinstance(x, Far) for x in outs]
    args = [pltpu.with_memory_space_constraint(x.value, pltpu.HBM) if isinstance(x, Far) else x for x in args]
    shapes = [x.value if isinstance(x, Far) else x for x in outs]
    buffers = [pltpu.VMEM(x.shape, x.dtype) for x, far in zip(args, far_in) if far]
    buffers += [pltpu.VMEM(x, F32) for x, far in zip(shapes, far_out) if far]
    moved = len(buffers)
    total_in, total_out = len(args), len(shapes)

    def whole(*refs):
        sems = refs[-1]
        refs = list(refs[:-1])
        spare = refs[total_in + total_out :][:moved]
        rest = refs[total_in + total_out + moved :]
        ins, results, at = {}, {}, 0
        for i, far in enumerate(far_in + far_out):
            if not far:
                continue
            remote, local = refs[i], spare[at]
            if i < total_in:
                ins[id(local)] = pltpu.make_async_copy(remote, local, sems.at[at])
            else:
                results[id(local)] = pltpu.make_async_copy(local, remote, sems.at[at])
            refs[i] = local
            at += 1
        copies = Copies(ins, results)
        kernel(copies, *refs[: total_in + total_out], *rest)
        for copy in results.values():
            copy.wait()

    far_spec = pl.BlockSpec(memory_space=pltpu.HBM)
    in_specs = [SM if i < scalars else (far_spec if far else VM) for i, far in enumerate(far_in)]
    return pl.pallas_call(
        whole,
        out_shape=tuple(
            pltpu.HBM(shape, F32) if far else jax.ShapeDtypeStruct(shape, F32) for shape, far in zip(shapes, far_out)
        ),
        in_specs=in_specs,
        out_specs=tuple(far_spec if far else VM for far in far_out),
        scratch_shapes=buffers + [x if x is SPOTS else pltpu.VMEM(x, F32) for x in scratch] + [pltpu.SemaphoreType.DMA((max(moved, 1),))],
        compiler_params=pltpu.CompilerParams(vmem_limit_bytes=limit * 1024 * 1024),
        name=name,
    )(*args)


def length(axes):
    return functools.reduce(lambda a, b: a * b, [lax.axis_size(axis) for axis in axes])


def from_before(value, axes):
    return lax.ppermute(value, axes, [(i, i + 1) for i in range(length(axes) - 1)])


def from_after(value, axes):
    return lax.ppermute(value, axes, [(i + 1, i) for i in range(length(axes) - 1)])


def swap(value, axes):
    count = length(axes)
    return lax.ppermute(value, axes, [(i, count - 1 - i) for i in range(count)])


def share_over_x(share):
    near = swap(share, ("xl",))
    far = swap(share, ("xh",))
    cross = swap(share, ("xh", "xl"))
    at = lax.broadcasted_iota(jnp.int32, share.shape, 0)
    added = (share + near) + (far + cross)
    largest = jnp.maximum(jnp.maximum(share, near), jnp.maximum(far, cross))
    return jnp.where(at < DATA, added, largest)


def body(object_field, probe_modes, scan_offsets, measured):
    n = probe_modes.shape[-1]
    modes = probe_modes.shape[1]
    half = n // 2
    tile = object_field.shape[1]
    extent = tile + n
    blocks = extent // n
    positions = scan_offsets.shape[2]
    offsets = scan_offsets.reshape(positions, 2)
    amplitudes = measured.reshape(positions, n, n)
    tables = dft_pair(n)
    row = lax.axis_index(ROW)
    col = lax.axis_index(COL)
    info = jnp.stack(
        [
            lax.axis_index("core"),
            jnp.where(row == 0, half, 0),
            jnp.where(row == length(ROW) - 1, extent - half, extent),
            jnp.where(col == 0, half, 0),
            jnp.where(col == length(COL) - 1, extent - half, extent),
        ]
    ).astype(jnp.int32)

    tag = (offsets + 1).astype(F32).reshape(1, 2 * positions)
    tag_rows = jnp.pad(tag, ((0, 7), (0, n - 2 * positions)))
    tag_block = jnp.pad(tag[None], ((0, 1), (0, 7), (0, tile - 2 * positions)))
    upper = from_before(jnp.concatenate([object_field[:, tile - half :], tag_block], 1), ROW)
    lower = from_after(jnp.concatenate([object_field[:, :half], tag_block], 1), ROW)
    strip = (extent + 8, n)
    tall, left, right = call(
        join_rows_kernel, [(2, extent, tile), strip, strip], [], [Far(object_field), upper, lower, tag_rows], 0, "join_rows"
    )
    before = from_before(right, COL)
    after = from_after(left, COL)
    own = jnp.concatenate([upper[0, half : half + 1, :32], tag, lower[0, half : half + 1, :32]], 0)
    tags = jnp.concatenate([before[extent : extent + 3, :32], own, after[extent : extent + 3, :32]], 0)

    cells = (2, blocks, extent, n)
    canvas = (1, blocks + 2, extent + 2 * n, n)
    grads = (2 * modes + 1, n, n)
    packed = (PARTS * CHUNK, n)
    band = (2, n, extent)
    probes = probe_modes
    tables = [Far(x) for x in tables]
    amplitudes = Far(amplitudes)
    for sweep in range(ITERS):
        last = sweep == ITERS - 1
        bands = [(2, half, extent), (2, tile, extent), (2, half, extent)] if last else [band] * 3
        outs = [Far(x) for x in bands] + [packed, packed, Far(cells)]
        if sweep == 0:
            args = [offsets, info, tall, before, after, probes, amplitudes, *tables]
            top, mid, low, keep, send, cells_now = call(first_kernel, outs, [cells, grads], args, 2, "first_sweep")
        else:
            held = [Far(x) for x in (cells_now, *sums, light)]
            args = [offsets, info, *held, mine, other, Far(probes), amplitudes, *tables]
            top, mid, low, keep, send, cells_now, probes = call(
                next_kernel, outs + [Far(probes.shape)], [cells, grads], args, 2, "next_sweep"
            )
        received = swap(send, ("core",))
        received, top, low, probes = lax.optimization_barrier((received, top, low, probes))
        parts = lax.all_to_all(keep + received, RING, 0, 0, tiled=True)
        light, peak = call(light_kernel, [Far(canvas), (8, n)], [SPOTS], [tags, Far(probes)], 1, "light")
        upper = from_before(low, ROW)
        lower = from_after(top, ROW)
        parts, upper, lower = lax.optimization_barrier((parts, upper, lower))
        share = call(share_kernel, [(CHUNK, n)], [], [parts, peak], 0, "share")[0]
        share = share_over_x(share)
        copies = jnp.broadcast_to(share[None], (PARTS,) + share.shape).reshape(packed)
        light, copies = lax.optimization_barrier((light, copies))
        mine = lax.all_to_all(copies, RING, 0, 0, tiled=True)
        if last:
            outs = [Far((2, tile, extent)), Far((tile, n)), Far((tile, n))]
            args = [Far(x) for x in (mid, upper, lower)]
            sums, left, right = call(fold_inner_kernel, outs, [], args, 0, "fold_inner")
            sums = [sums]
        else:
            side = (2, extent, n)
            outs = [Far(x) for x in (band, band, side, side)]
            args = [Far(x) for x in (top, low, mid, upper, lower)]
            top, low, left, right = call(fold_kernel, outs, [], args, 0, "fold_rows")
            sums = [top, mid, low]
            args = [tags, Far(probes), Far(light)]
            light = call(more_light_kernel, [Far(canvas)], [SPOTS], args, 1, "more_light")[0]
        left, right = from_before(right, COL), from_after(left, COL)
        mine, left, right, light = lax.optimization_barrier((mine, left, right, light))
        sums += [left, right]
        other = swap(mine, ("core",))
    held = [Far(x) for x in (cells_now, *sums, light)]
    args = [info, *held, mine, other, Far(probes)]
    return call(last_kernel, [object_field.shape, probes.shape], [grads], args, 1, "last_update")


def solution(mesh):
    names = tuple(name for name, _ in SPLIT)
    sizes = tuple(size for _, size in SPLIT)
    fine = Mesh(mesh.devices.reshape(sizes), names)
    return jax.shard_map(
        body,
        mesh=fine,
        in_specs=(
            P(None, ROW, COL),
            P(),
            P(ROW, COL, None, None),
            P(ROW, COL, None, None, None),
        ),
        out_specs=(P(None, ROW, COL), P()),
        check_vma=False,
    )
```

```python
import functools

import jax
import jax.numpy as jnp
import numpy as np
from jax import lax
from jax.experimental import pallas as pl
from jax.experimental.pallas import tpu as pltpu
from jax.sharding import Mesh, PartitionSpec as P

ITERS = 2
BATCH = 4
SPLIT = (("y", 4), ("xh", 2), ("core", 2), ("xl", 2), ("z", 8))
ROW = ("y", "xh", "core")
COL = ("xl", "z")
RING = ("y", "z")
PARTS = 32
CHUNK = 24
DATA = 18

VM = pl.BlockSpec(memory_space=pltpu.VMEM)
SM = pl.BlockSpec(memory_space=pltpu.SMEM)
F32 = jnp.float32
SPOTS = pltpu.SMEM((9 * 16 + 4, 2), jnp.int32)


def dft_pair(n):
    index = np.arange(n)
    angle = (index[:, None] * index[None, :] % n) * (2.0 * np.pi / n)
    c = np.cos(angle) / np.sqrt(n)
    s = np.sin(angle) / np.sqrt(n)
    forward = np.block([[c, s], [-s, c]])
    backward = np.block([[c, -s], [s, c]])
    return jnp.asarray(forward, jnp.bfloat16), jnp.asarray(backward, jnp.bfloat16)


def ordered(odd, first, second):
    return jnp.where(odd, first, second), jnp.where(odd, second, first)


def total(values):
    return functools.reduce(jnp.add, values)


def place(canvas, ch, where, lane, value):
    u, k, s = where
    n = value.shape[0]
    rolled = pltpu.roll(value, s, 1)
    canvas[ch, k, pl.ds(u, n), :] += jnp.where(lane >= s, rolled, 0.0)
    canvas[ch, k + 1, pl.ds(u, n), :] += jnp.where(lane >= s, 0.0, rolled)


def sweep_positions(copies, off_ref, probe_ref, meas_ref, fwd_ref, bwd_ref, cells, canvas, grads):
    modes = probe_ref.shape[1]
    n = probe_ref.shape[2]
    grads[...] = jnp.zeros_like(grads)
    lane = lax.broadcasted_iota(jnp.int32, (n, n), 1)

    def window(ch, where):
        u, k, s = where
        left = cells[ch, k, pl.ds(u, n), :]
        right = cells[ch, k + 1, pl.ds(u, n), :]
        return pltpu.roll(jnp.where(lane >= s, left, right), n - s, 1)

    def transform(field, left, right):
        sec = jnp.dot(left, field, preferred_element_type=F32).astype(jnp.bfloat16)
        parts = [slice(m * n, (m + 1) * n) for m in range(modes)]
        rows = [jnp.concatenate([sec[:n, part], sec[n:, part]], 1) for part in parts]
        return jnp.dot(jnp.concatenate(rows, 0), right, preferred_element_type=F32)

    def paired(re_parts, im_parts):
        re_all = jnp.concatenate([x.astype(jnp.bfloat16) for x in re_parts], 1)
        im_all = jnp.concatenate([x.astype(jnp.bfloat16) for x in im_parts], 1)
        return jnp.concatenate([re_all, im_all], 0)

    def split(wave):
        return [(wave[m * n : (m + 1) * n, :n], wave[m * n : (m + 1) * n, n:]) for m in range(modes)]

    def spot(q):
        u = off_ref[q, 0]
        v = off_ref[q, 1]
        return u, v // n, lax.rem(v, n)

    def step(i, carry):
        copies.need_part(meas_ref, i)
        probes = [(probe_ref[0, m], probe_ref[1, m]) for m in range(modes)]
        spots = [spot(i * BATCH + j) for j in range(BATCH)]
        wins = [(window(0, where), window(1, where)) for where in spots]
        exits = []
        for w_re, w_im in wins:
            re_parts = [p_re * w_re - p_im * w_im for p_re, p_im in probes]
            im_parts = [p_re * w_im + p_im * w_re for p_re, p_im in probes]
            exits.append(paired(re_parts, im_parts))
        fars = [split(transform(x, fwd_ref[...], bwd_ref[...])) for x in exits]
        corrected = []
        for j, far in enumerate(fars):
            power = total([re * re + im * im for re, im in far])
            raised = power + 1.0
            root = lax.rsqrt(raised)
            root = root * (1.5 - 0.5 * raised * root * root)
            scale = meas_ref[i * BATCH + j] * root
            corrected.append(paired([re * scale for re, _ in far], [im * scale for _, im in far]))
        backs = [split(transform(x, bwd_ref[...], fwd_ref[...])) for x in corrected]
        for where, back in zip(spots, backs):
            place(canvas, 0, where, lane, total([p[0] * b[0] + p[1] * b[1] for p, b in zip(probes, back)]))
            place(canvas, 1, where, lane, total([p[0] * b[1] - p[1] * b[0] for p, b in zip(probes, back)]))
        for m in range(modes):
            pairs = [(w, back[m]) for w, back in zip(wins, backs)]
            grads[m] += total([w[0] * b[0] + w[1] * b[1] for w, b in pairs])
            grads[modes + m] += total([w[0] * b[1] - w[1] * b[0] for w, b in pairs])
        grads[2 * modes] += total([w[0] * w[0] + w[1] * w[1] for w in wins])
        return carry

    lax.fori_loop(0, meas_ref.shape[0] // BATCH, step, 0)


def pack_half(grads, half, out_ref):
    planes = grads.shape[0]
    out_ref[...] = jnp.zeros_like(out_ref)
    for c in range(planes):
        for t in range(2):
            out_ref[pl.ds(2 * c + t, PARTS, stride=CHUNK), :] = grads[
                c, pl.ds(half * 2 * PARTS + t, PARTS, stride=2), :
            ]


def unpack_half(in_ref, half, grads):
    planes = grads.shape[0]
    for c in range(planes):
        for t in range(2):
            grads[c, pl.ds(half * 2 * PARTS + t, PARTS, stride=2), :] = in_ref[
                pl.ds(2 * c + t, PARTS, stride=CHUNK), :
            ]


def finish(copies, at_ref, canvas, grads, first_ref, second_ref, mid_ref, keep_ref, send_ref):
    band = first_ref.shape[2]
    far = canvas.shape[2] - band
    low = (1 - at_ref[5]) * far
    copies.send(canvas.at[:, :, pl.ds(pl.multiple_of(low, 8), band)], first_ref)
    copies.send(canvas.at[:, :, pl.ds(pl.multiple_of(far - low, 8), band)], second_ref)
    copies.send(canvas.at[:, :, band : band + mid_ref.shape[2]], mid_ref)
    for core in range(2):

        @pl.when(at_ref[0] == core)
        def _():
            pack_half(grads, core, keep_ref)
            pack_half(grads, 1 - core, send_ref)


def brightness(probe_ref):
    return jnp.sum(probe_ref[0] * probe_ref[0] + probe_ref[1] * probe_ref[1], axis=0)


def join_rows_kernel(
    copies, at_ref, obj_ref, row_a_ref, row_b_ref, tag_ref, tall_ref, col_a_ref, col_b_ref, tags_ref
):
    band = row_a_ref.shape[1] - 8
    size = obj_ref.shape[1]
    n = col_a_ref.shape[1]
    extent = tall_ref.shape[1]
    upper, lower = ordered(at_ref[5] == 1, row_a_ref[...], row_b_ref[...])
    tall_ref[:, :band] = upper[:, :band]
    tall_ref[:, band + size :] = lower[:, :band]
    tags_ref[...] = jnp.zeros_like(tags_ref)
    tags_ref[:1] = upper[0, band : band + 1, :n]
    tags_ref[1:2] = tag_ref[:1]
    tags_ref[2:3] = lower[0, band : band + 1, :n]
    copies.need(obj_ref)
    tall_ref[:, band : band + size] = obj_ref[...]
    lane = lax.broadcasted_iota(jnp.int32, (extent, n), 1)
    left = jnp.where(lane < band, tall_ref[0, :, :n], pltpu.roll(tall_ref[1, :, :n], band, 1))
    right = jnp.where(lane < band, pltpu.roll(tall_ref[0, :, size - n :], band, 1), tall_ref[1, :, size - n :])
    col_a_ref[:extent], col_b_ref[:extent] = ordered(at_ref[6] == 1, left, right)
    col_a_ref[extent:] = tags_ref[...]
    col_b_ref[extent:] = tags_ref[...]


def first_kernel(
    copies, off_ref, at_ref, tall_ref, col_a_ref, col_b_ref, probe_ref, meas_ref, fwd_ref, bwd_ref,
    first_ref, second_ref, mid_ref, keep_ref, send_ref, cells, bright_ref, canvas, grads,
):
    n = probe_ref.shape[2]
    half = n // 2
    extent = tall_ref.shape[1]
    lane = lax.broadcasted_iota(jnp.int32, (extent, n), 1)
    canvas[...] = jnp.zeros_like(canvas)
    bright_ref[...] = brightness(probe_ref)
    copies.ready(bright_ref)
    before, after = ordered(at_ref[6] == 1, col_a_ref[:extent], col_b_ref[:extent])
    strips = [
        (before, pltpu.roll(after, half, 1)),
        (pltpu.roll(before, half, 1), after),
    ]
    for ch in range(2):
        inner = [pltpu.roll(tall_ref[ch, :, k * n : (k + 1) * n], half, 1) for k in range(2)]
        row = [strips[ch][0], *inner, strips[ch][1]]
        for k in range(3):
            cells[ch, k] = jnp.where(lane < half, row[k], row[k + 1])
    copies.ready(cells)
    copies.need(fwd_ref, bwd_ref)
    sweep_positions(copies, off_ref, probe_ref, meas_ref, fwd_ref, bwd_ref, cells, canvas, grads)
    finish(copies, at_ref, canvas, grads, first_ref, second_ref, mid_ref, keep_ref, send_ref)


def light_peak(mine_ref, other_ref):
    best = [jnp.max(ref[pl.ds(DATA, PARTS, stride=CHUNK), :]) for ref in (mine_ref, other_ref)]
    return jnp.maximum(best[0], best[1])


def update_probes(at_ref, mine_ref, other_ref, probe_ref, grads, new_probe_ref):
    modes = probe_ref.shape[1]
    for core in range(2):

        @pl.when(at_ref[0] == core)
        def _():
            unpack_half(mine_ref, core, grads)
            unpack_half(other_ref, 1 - core, grads)

    density = grads[2 * modes]
    scale = 1.0 / (density + 0.1 * jnp.max(density))
    for part in range(2):
        for m in range(modes):
            old = probe_ref[part, m]
            new_probe_ref[part, m] = old + (grads[part * modes + m] - old * density) * scale


def updated(old, sums, light, peak):
    scale = 1.0 / (light + 0.1 * peak)
    return [old[ch] + (sums[ch] - old[ch] * light) * scale for ch in range(2)]


def next_kernel(
    copies, off_ref, at_ref, obj_ref, top_ref, mid_ref, low_ref, col_a_ref, col_b_ref, light_ref,
    mine_ref, other_ref, probe_ref, meas_ref, fwd_ref, bwd_ref,
    first_ref, second_ref, new_mid_ref, keep_ref, send_ref, new_obj_ref, bright_ref, new_probe_ref,
    canvas, grads,
):
    n = probe_ref.shape[2]
    blocks = obj_ref.shape[1]
    canvas[...] = jnp.zeros_like(canvas)
    peak = light_peak(mine_ref, other_ref)
    copies.need(probe_ref)
    update_probes(at_ref, mine_ref, other_ref, probe_ref, grads, new_probe_ref)
    copies.ready(new_probe_ref)
    bright_ref[...] = brightness(new_probe_ref)
    copies.ready(bright_ref)
    copies.need(obj_ref, top_ref, mid_ref, low_ref, col_a_ref, col_b_ref, light_ref)
    for j, ref in enumerate((top_ref, mid_ref, low_ref)):
        rows = slice(j * n, (j + 1) * n)
        row = lax.broadcasted_iota(jnp.int32, (n, n), 0) + j * n
        row_ok = (row >= at_ref[1]) & (row < at_ref[2])
        for k in range(blocks):
            col = lax.broadcasted_iota(jnp.int32, (n, n), 1) + k * n
            inside = row_ok & (col >= at_ref[3]) & (col < at_ref[4])
            sums = ref[:, k]
            if k in (0, blocks - 1):
                sides = ordered(at_ref[6] == 1, col_a_ref[:, rows], col_b_ref[:, rows])
                sums = sums + sides[k > 0]
            new = updated(obj_ref[:, k, rows], sums, light_ref[k, rows], peak)
            for ch in range(2):
                new_obj_ref[ch, k, rows] = jnp.where(inside, new[ch], 0.0)
    copies.ready(new_obj_ref)
    copies.need(fwd_ref, bwd_ref)
    sweep_positions(copies, off_ref, new_probe_ref, meas_ref, fwd_ref, bwd_ref, new_obj_ref, canvas, grads)
    finish(copies, at_ref, canvas, grads, first_ref, second_ref, new_mid_ref, keep_ref, send_ref)


def last_kernel(
    copies, at_ref, obj_ref, sums_ref, col_a_ref, col_b_ref, light_ref, mine_ref, other_ref, probe_ref,
    out_ref, new_probe_ref, grads,
):
    n = probe_ref.shape[2]
    half = n // 2
    blocks = obj_ref.shape[1]
    tile = out_ref.shape[1]
    inner = slice(half, half + tile)
    copies.need(probe_ref)
    update_probes(at_ref, mine_ref, other_ref, probe_ref, grads, new_probe_ref)
    copies.ready(new_probe_ref)
    copies.need(obj_ref, sums_ref, col_a_ref, col_b_ref, light_ref)
    left, right = ordered(at_ref[6] == 1, col_a_ref[...], col_b_ref[...])
    peak = light_peak(mine_ref, other_ref)
    lane = lax.broadcasted_iota(jnp.int32, (tile, n), 1)
    rolled = []
    for k in range(blocks):
        sums = [sums_ref[ch, k] for ch in range(2)]
        if k == 0:
            sums[0] = sums[0] + jnp.where(lane < half, 0.0, left)
            sums[1] = sums[1] + jnp.where(lane < half, 0.0, pltpu.roll(left, half, 1))
        elif k == blocks - 1:
            sums[0] = sums[0] + jnp.where(lane < half, right, 0.0)
            sums[1] = sums[1] + jnp.where(lane < half, pltpu.roll(right, half, 1), 0.0)
        new = updated(obj_ref[:, k, inner], sums, light_ref[k, inner], peak)
        rolled.append([pltpu.roll(x, half, 1) for x in new])
    for k in range(blocks - 1):
        for ch in range(2):
            out_ref[ch, :, k * n : (k + 1) * n] = jnp.where(lane < half, rolled[k][ch], rolled[k + 1][ch])
    copies.ready(out_ref)


def fold_kernel(
    copies, at_ref, first_ref, second_ref, mid_ref, row_a_ref, row_b_ref, top_ref, low_ref, col_a_ref, col_b_ref
):
    n = col_a_ref.shape[2]
    last = top_ref.shape[1] - 1
    copies.need(first_ref, second_ref, mid_ref, row_a_ref, row_b_ref)
    top_ref[...], low_ref[...] = ordered(
        at_ref[5] == 1, first_ref[...] + row_a_ref[...], second_ref[...] + row_b_ref[...]
    )
    for j, ref in enumerate((top_ref, mid_ref, low_ref)):
        rows = slice(j * n, (j + 1) * n)
        col_a_ref[:, rows], col_b_ref[:, rows] = ordered(at_ref[6] == 1, ref[:, 0], ref[:, last])
    copies.ready(col_a_ref, col_b_ref, top_ref, low_ref)


def fold_inner_kernel(copies, at_ref, mid_ref, row_a_ref, row_b_ref, sums_ref, col_a_ref, col_b_ref):
    n = col_a_ref.shape[1]
    band = row_a_ref.shape[2]
    tile = mid_ref.shape[2]
    last = mid_ref.shape[1] - 1
    copies.need(mid_ref, row_a_ref, row_b_ref)
    upper, lower = ordered(at_ref[5] == 1, row_a_ref[...], row_b_ref[...])
    sums_ref[:, :, :band] = mid_ref[:, :, :band] + upper
    sums_ref[:, :, band : tile - band] = mid_ref[:, :, band : tile - band]
    sums_ref[:, :, tile - band :] = mid_ref[:, :, tile - band :] + lower
    lane = lax.broadcasted_iota(jnp.int32, (tile, n), 1)
    left = jnp.where(lane < band, sums_ref[0, 0], pltpu.roll(sums_ref[1, 0], band, 1))
    right = jnp.where(lane < band, pltpu.roll(sums_ref[1, last], band, 1), sums_ref[0, last])
    col_a_ref[...], col_b_ref[...] = ordered(at_ref[6] == 1, left, right)
    copies.ready(col_a_ref, col_b_ref, sums_ref)


def place_lights(tag_ref, bright_ref, canvas, spots, rim, tile):
    n = bright_ref.shape[1]
    half = n // 2
    group = 4
    lane = lax.broadcasted_iota(jnp.int32, (n, n), 1)
    count = jnp.int32(0)
    for t in range(9):
        if rim and t == 4:
            continue
        down, across = t % 3 - 1, t // 3 - 1

        def gather(p, count):
            u = tag_ref[t, 2 * p]
            v = tag_ref[t, 2 * p + 1]
            held = u > 0
            u = u + (n - 1 + down * tile)
            v = v + (n - 1 + across * tile)
            inner = (u > half) & (u < tile + n + half) & (v > half) & (v < tile + n + half)
            if rim:
                held = held & ~inner & (u > 0) & (u < tile + 2 * n) & (v > 0) & (v < tile + 2 * n)
            else:
                held = held & inner
            spots[count, 0] = u
            spots[count, 1] = v
            return count + held.astype(jnp.int32)

        count = lax.fori_loop(0, tag_ref.shape[1] // 2, gather, count, unroll=16)
    for j in range(group):
        spots[count + j, 0] = 0
        spots[count + j, 1] = 0
    canvas[...] = jnp.zeros_like(canvas)
    value = bright_ref[...]

    def step(i, carry):
        held = []
        for j in range(group):
            u = spots[i * group + j, 0]
            v = spots[i * group + j, 1]
            s = lax.rem(v, n)
            held.append((u, v // n, s, pltpu.roll(value, s, 1)))
        for u, k, s, rolled in held:
            canvas[k, pl.ds(u, n), :] += jnp.where(lane >= s, rolled, 0.0)
            canvas[k + 1, pl.ds(u, n), :] += jnp.where(lane >= s, 0.0, rolled)
        return carry

    lax.fori_loop(0, (count + group - 1) // group, step, 0)


def light_kernel(copies, tag_ref, bright_ref, light_ref, peak_ref, canvas, spots):
    n = bright_ref.shape[1]
    half = n // 2
    blocks, extent = light_ref.shape[:2]
    copies.need(bright_ref)
    place_lights(tag_ref, bright_ref, canvas, spots, False, extent - n)
    light_ref[...] = canvas[1 : 1 + blocks, n : n + extent]
    copies.ready(light_ref)
    lane = lax.broadcasted_iota(jnp.int32, (extent - n, n), 1)
    best = None
    for k in range(blocks):
        mine = light_ref[k, half : extent - half]
        if k == 0:
            mine = jnp.where(lane >= half, mine, 0.0)
        elif k == blocks - 1:
            mine = jnp.where(lane < half, mine, 0.0)
        best = mine if best is None else jnp.maximum(best, mine)
    peak_ref[...] = jnp.full(peak_ref.shape, jnp.max(best), F32)


def more_light_kernel(copies, tag_ref, bright_ref, light_ref, all_ref, canvas, spots):
    n = bright_ref.shape[1]
    blocks, extent = light_ref.shape[:2]
    copies.need(bright_ref)
    place_lights(tag_ref, bright_ref, canvas, spots, True, extent - n)
    copies.need(light_ref)
    all_ref[...] = light_ref[...] + canvas[1 : 1 + blocks, n : n + extent]
    copies.ready(all_ref)


def share_kernel(copies, parts_ref, peak_ref, out_ref):
    share = parts_ref[:CHUNK]
    for s in range(1, PARTS):
        share = share + parts_ref[s * CHUNK : (s + 1) * CHUNK]
    row = lax.broadcasted_iota(jnp.int32, share.shape, 0)
    out_ref[...] = jnp.where(row < DATA, share, peak_ref[:1])


class Far:
    def __init__(self, value, parts=1):
        self.value = value
        self.parts = parts


class Raw(Far):
    pass


class Copies:
    def __init__(self):
        self.ins = {}
        self.outs = {}
        self.sems = {}
        self.sent = []

    def need(self, *refs):
        for ref in refs:
            copy = self.ins.pop(id(ref), None)
            if copy is not None:
                copy(0).wait()

    def need_part(self, ref, i):
        if id(ref) in self.ins:
            self.ins[id(ref)](i).wait()

    def ready(self, *refs):
        for ref in refs:
            copy = self.outs.get(id(ref))
            if copy is not None:
                copy.start()
                self.sent.append(copy)

    def send(self, local, remote):
        copy = pltpu.make_async_copy(local, remote, self.sems[id(remote)])
        copy.start()
        self.sent.append(copy)


def part_copy(remote, local, sems, first, parts):
    size = local.shape[0] // parts

    def copy(i):
        rows = pl.ds(i * size, size)
        return pltpu.make_async_copy(remote.at[rows], local.at[rows], sems.at[first + i])

    return copy


def call(kernel, outs, scratch, args, scalars, name, limit=24):
    info = list(args) + list(outs)
    split = len(args)
    values = [x.value if isinstance(x, Far) else x for x in info]
    far = [isinstance(x, Far) for x in info]
    raw = [isinstance(x, Raw) for x in info]
    buffers, sem_at, count = [], {}, 0
    for i, value in enumerate(values):
        if far[i]:
            sem_at[i] = count
            count += info[i].parts
            if not raw[i]:
                buffers.append(pltpu.VMEM(value.shape, value.dtype) if i < split else pltpu.VMEM(value, F32))

    def whole(*refs):
        sems = refs[-1]
        refs = list(refs[:-1])
        spare = iter(refs[len(info) : len(info) + len(buffers)])
        rest = refs[len(info) + len(buffers) :]
        copies = Copies()
        for i in sem_at:
            first = sem_at[i]
            if raw[i]:
                copies.sems[id(refs[i])] = sems.at[first]
                continue
            remote, local = refs[i], next(spare)
            refs[i] = local
            if i < split:
                copies.ins[id(local)] = part_copy(remote, local, sems, first, info[i].parts)
                for j in range(info[i].parts):
                    copies.ins[id(local)](j).start()
            else:
                copies.outs[id(local)] = pltpu.make_async_copy(local, remote, sems.at[first])
        kernel(copies, *refs[: len(info)], *rest)
        for copy in copies.sent:
            copy.wait()

    far_spec = pl.BlockSpec(memory_space=pltpu.HBM)
    specs = [SM if i < scalars else (far_spec if far[i] else VM) for i in range(len(info))]
    operands = [
        pltpu.with_memory_space_constraint(x, pltpu.HBM) if is_far else x for x, is_far in zip(values[:split], far)
    ]
    return pl.pallas_call(
        whole,
        out_shape=tuple(
            pltpu.HBM(x, F32) if is_far else jax.ShapeDtypeStruct(x, F32) for x, is_far in zip(values[split:], far[split:])
        ),
        in_specs=specs[:split],
        out_specs=tuple(specs[split:]),
        scratch_shapes=buffers
        + [x if x is SPOTS else pltpu.VMEM(x, F32) for x in scratch]
        + [pltpu.SemaphoreType.DMA((max(count, 1),))],
        compiler_params=pltpu.CompilerParams(vmem_limit_bytes=limit * 1024 * 1024),
        name=name,
    )(*operands)


def length(axes):
    return functools.reduce(lambda a, b: a * b, [lax.axis_size(axis) for axis in axes])


def exchange(first, second, axes):
    count = length(axes)
    first = lax.ppermute(first, axes, [(i, i ^ 1) for i in range(count)])
    pairs = [(i, i + 1) for i in range(1, count - 1, 2)]
    second = lax.ppermute(second, axes, pairs + [(j, i) for i, j in pairs])
    return first, second


def swap(value, axes):
    count = length(axes)
    return lax.ppermute(value, axes, [(i, count - 1 - i) for i in range(count)])


def share_over_x(share):
    near = swap(share, ("xl",))
    far = swap(share, ("xh",))
    cross = swap(share, ("xh", "xl"))
    at = lax.broadcasted_iota(jnp.int32, share.shape, 0)
    added = (share + near) + (far + cross)
    largest = jnp.maximum(jnp.maximum(share, near), jnp.maximum(far, cross))
    return jnp.where(at < DATA, added, largest)


def body(object_field, probe_modes, scan_offsets, measured):
    n = probe_modes.shape[-1]
    modes = probe_modes.shape[1]
    half = n // 2
    tile = object_field.shape[1]
    extent = tile + n
    blocks = extent // n
    positions = scan_offsets.shape[2]
    offsets = scan_offsets.reshape(positions, 2)
    amplitudes = measured.reshape(positions, n, n)
    tables = dft_pair(n)
    row = lax.axis_index(ROW)
    col = lax.axis_index(COL)
    info = jnp.stack(
        [
            lax.axis_index("core"),
            jnp.where(row == 0, half, 0),
            jnp.where(row == length(ROW) - 1, extent - half, extent),
            jnp.where(col == 0, half, 0),
            jnp.where(col == length(COL) - 1, extent - half, extent),
            row % 2,
            col % 2,
        ]
    ).astype(jnp.int32)

    tag = (offsets + 1).astype(F32).reshape(1, 2 * positions)
    tag_rows = jnp.pad(tag, ((0, 7), (0, n - 2 * positions)))
    tag_block = jnp.pad(tag[None], ((0, 1), (0, 7), (0, tile - 2 * positions)))
    low = (1 - row % 2) * (tile - half)
    first = lax.dynamic_slice_in_dim(object_field, low, half, 1)
    second = lax.dynamic_slice_in_dim(object_field, tile - half - low, half, 1)
    row_a, row_b = exchange(*(jnp.concatenate([x, tag_block], 1) for x in (first, second)), ROW)
    strip = (extent + 8, n)
    tall, col_a, col_b, own = call(
        join_rows_kernel,
        [(2, extent, tile), strip, strip, (8, n)],
        [],
        [info, Far(object_field), row_a, row_b, tag_rows],
        1,
        "join_rows",
    )
    col_a, col_b = exchange(col_a, col_b, COL)
    odd = col % 2 == 1
    before, after = ordered(odd, col_a[extent : extent + 3, :32], col_b[extent : extent + 3, :32])
    tags = jnp.concatenate([before, own[:3, :32], after], 0)
    tags = tags.astype(jnp.int32)

    cells = (2, blocks, extent, n)
    canvas = (blocks + 2, extent + 2 * n, n)
    lights = (blocks, extent, n)
    grads = (2 * modes + 1, n, n)
    packed = (PARTS * CHUNK, n)
    band = (2, blocks, n, n)
    probes = probe_modes
    tables = [Far(x) for x in tables]
    amplitudes = Far(amplitudes, positions // BATCH)
    for sweep in range(ITERS):
        last = sweep == ITERS - 1
        bands = [(2, blocks, x, n) for x in ((half, half, tile) if last else (n, n, n))]
        outs = [Raw(x) for x in bands] + [packed, packed, Far(cells), Far((n, n))]
        if sweep == 0:
            args = [offsets, info, tall, col_a, col_b, probes, amplitudes, *tables]
            first, second, mid, keep, send, cells_now, bright = call(first_kernel, outs, [cells, grads], args, 2, "first_sweep")
        else:
            held = [Far(x) for x in (cells_now, *sums, light)]
            args = [offsets, info, *held, mine, other, Far(probes), amplitudes, *tables]
            first, second, mid, keep, send, cells_now, bright, probes = call(
                next_kernel, outs + [Far(probes.shape)], [cells, grads], args, 2, "next_sweep"
            )
        received = swap(send, ("core",))
        received, first, second, bright = lax.optimization_barrier((received, first, second, bright))
        parts = lax.all_to_all(keep + received, RING, 0, 0, tiled=True)
        light, peak = call(light_kernel, [Far(lights), (8, n)], [canvas, SPOTS], [tags, Far(bright)], 1, "light")
        row_a, row_b = exchange(first, second, ROW)
        parts, row_a, row_b = lax.optimization_barrier((parts, row_a, row_b))
        share = call(share_kernel, [(CHUNK, n)], [], [parts, peak], 0, "share")[0]
        share = share_over_x(share)
        copies = jnp.broadcast_to(share[None], (PARTS,) + share.shape).reshape(packed)
        light, copies = lax.optimization_barrier((light, copies))
        mine = lax.all_to_all(copies, RING, 0, 0, tiled=True)
        if last:
            outs = [Far((2, blocks, tile, n)), Far((tile, n)), Far((tile, n))]
            args = [info] + [Far(x) for x in (mid, row_a, row_b)]
            sums, col_a, col_b = call(fold_inner_kernel, outs, [], args, 1, "fold_inner")
            sums = [sums]
        else:
            side = (2, extent, n)
            outs = [Far(x) for x in (band, band, side, side)]
            args = [info] + [Far(x) for x in (first, second, mid, row_a, row_b)]
            top, low, col_a, col_b = call(fold_kernel, outs, [], args, 1, "fold_rows")
            sums = [top, mid, low]
            args = [tags, Far(bright), Far(light)]
            light = call(more_light_kernel, [Far(lights)], [canvas, SPOTS], args, 1, "more_light")[0]
        col_a, col_b = exchange(col_a, col_b, COL)
        mine, col_a, col_b, light = lax.optimization_barrier((mine, col_a, col_b, light))
        sums += [col_a, col_b]
        other = swap(mine, ("core",))
    held = [Far(x) for x in (cells_now, *sums, light)]
    args = [info, *held, mine, other, Far(probes)]
    return call(last_kernel, [Far(object_field.shape), Far(probes.shape)], [grads], args, 1, "last_update")


def solution(mesh):
    names = tuple(name for name, _ in SPLIT)
    sizes = tuple(size for _, size in SPLIT)
    fine = Mesh(mesh.devices.reshape(sizes), names)
    return jax.shard_map(
        body,
        mesh=fine,
        in_specs=(
            P(None, ROW, COL),
            P(),
            P(ROW, COL, None, None),
            P(ROW, COL, None, None, None),
        ),
        out_specs=(P(None, ROW, COL), P()),
        check_vma=False,
    )
```

```python
import functools

import jax
import jax.numpy as jnp
import numpy as np
from jax import lax
from jax.experimental import pallas as pl
from jax.experimental.pallas import tpu as pltpu
from jax.sharding import Mesh, PartitionSpec as P

ITERS = 2
BATCH = 4
SPLIT = (("y", 4), ("xh", 2), ("core", 2), ("xl", 2), ("z", 8))
ROW = ("y", "xh", "core")
COL = ("xl", "z")
RING = ("y", "z")
PARTS = 32
CHUNK = 24
DATA = 18

VM = pl.BlockSpec(memory_space=pltpu.VMEM)
SM = pl.BlockSpec(memory_space=pltpu.SMEM)
F32 = jnp.float32
SPOTS = pltpu.SMEM((9 * 16 + 4, 2), jnp.int32)


def dft_pair(n):
    index = np.arange(n)
    angle = (index[:, None] * index[None, :] % n) * (2.0 * np.pi / n)
    c = np.cos(angle) / np.sqrt(n)
    s = np.sin(angle) / np.sqrt(n)
    forward = np.block([[c, s], [-s, c]])
    backward = np.block([[c, -s], [s, c]])
    return jnp.asarray(forward, jnp.bfloat16), jnp.asarray(backward, jnp.bfloat16)


def ordered(odd, first, second):
    return jnp.where(odd, first, second), jnp.where(odd, second, first)


def total(values):
    return functools.reduce(jnp.add, values)


def place(canvas, ch, where, lane, value):
    u, k, s = where
    n = value.shape[0]
    rolled = pltpu.roll(value, s, 1)
    canvas[ch, k, pl.ds(u, n), :] += jnp.where(lane >= s, rolled, 0.0)
    canvas[ch, k + 1, pl.ds(u, n), :] += jnp.where(lane >= s, 0.0, rolled)


def sweep_positions(copies, off_ref, probe_ref, meas_ref, fwd_ref, bwd_ref, cells, canvas, grads):
    modes = probe_ref.shape[1]
    n = probe_ref.shape[2]
    grads[...] = jnp.zeros_like(grads)
    lane = lax.broadcasted_iota(jnp.int32, (n, n), 1)

    def window(ch, where):
        u, k, s = where
        left = cells[ch, k, pl.ds(u, n), :]
        right = cells[ch, k + 1, pl.ds(u, n), :]
        return pltpu.roll(jnp.where(lane >= s, left, right), n - s, 1)

    def transform(field, left, right):
        sec = jnp.dot(left, field, preferred_element_type=F32).astype(jnp.bfloat16)
        parts = [slice(m * n, (m + 1) * n) for m in range(modes)]
        rows = [jnp.concatenate([sec[:n, part], sec[n:, part]], 1) for part in parts]
        return jnp.dot(jnp.concatenate(rows, 0), right, preferred_element_type=F32)

    def paired(re_parts, im_parts):
        re_all = jnp.concatenate([x.astype(jnp.bfloat16) for x in re_parts], 1)
        im_all = jnp.concatenate([x.astype(jnp.bfloat16) for x in im_parts], 1)
        return jnp.concatenate([re_all, im_all], 0)

    def split(wave):
        return [(wave[m * n : (m + 1) * n, :n], wave[m * n : (m + 1) * n, n:]) for m in range(modes)]

    def spot(q):
        u = off_ref[q, 0]
        v = off_ref[q, 1]
        return u, v // n, lax.rem(v, n)

    def step(i, carry):
        copies.need_part(meas_ref, i)
        probes = [(probe_ref[0, m], probe_ref[1, m]) for m in range(modes)]
        spots = [spot(i * BATCH + j) for j in range(BATCH)]
        wins = [(window(0, where), window(1, where)) for where in spots]
        exits = []
        for w_re, w_im in wins:
            re_parts = [p_re * w_re - p_im * w_im for p_re, p_im in probes]
            im_parts = [p_re * w_im + p_im * w_re for p_re, p_im in probes]
            exits.append(paired(re_parts, im_parts))
        fars = [split(transform(x, fwd_ref[...], bwd_ref[...])) for x in exits]
        corrected = []
        for j, far in enumerate(fars):
            power = total([re * re + im * im for re, im in far])
            raised = power + 1.0
            root = lax.rsqrt(raised)
            root = root * (1.5 - 0.5 * raised * root * root)
            scale = meas_ref[i * BATCH + j] * root
            corrected.append(paired([re * scale for re, _ in far], [im * scale for _, im in far]))
        backs = [split(transform(x, bwd_ref[...], fwd_ref[...])) for x in corrected]
        for where, back in zip(spots, backs):
            place(canvas, 0, where, lane, total([p[0] * b[0] + p[1] * b[1] for p, b in zip(probes, back)]))
            place(canvas, 1, where, lane, total([p[0] * b[1] - p[1] * b[0] for p, b in zip(probes, back)]))
        for m in range(modes):
            pairs = [(w, back[m]) for w, back in zip(wins, backs)]
            grads[m] += total([w[0] * b[0] + w[1] * b[1] for w, b in pairs])
            grads[modes + m] += total([w[0] * b[1] - w[1] * b[0] for w, b in pairs])
        grads[2 * modes] += total([w[0] * w[0] + w[1] * w[1] for w in wins])
        return carry

    lax.fori_loop(0, meas_ref.shape[0] // BATCH, step, 0)


def pack_half(grads, half, out_ref):
    planes = grads.shape[0]
    out_ref[...] = jnp.zeros_like(out_ref)
    for c in range(planes):
        for t in range(2):
            out_ref[pl.ds(2 * c + t, PARTS, stride=CHUNK), :] = grads[
                c, pl.ds(half * 2 * PARTS + t, PARTS, stride=2), :
            ]


def unpack_half(in_ref, half, grads):
    planes = grads.shape[0]
    for c in range(planes):
        for t in range(2):
            grads[c, pl.ds(half * 2 * PARTS + t, PARTS, stride=2), :] = in_ref[
                pl.ds(2 * c + t, PARTS, stride=CHUNK), :
            ]


def finish(copies, at_ref, canvas, grads, first_ref, second_ref, mid_ref, keep_ref, send_ref):
    band = first_ref.shape[2]
    far = canvas.shape[2] - band
    low = (1 - at_ref[5]) * far
    copies.send(canvas.at[:, :, pl.ds(pl.multiple_of(low, 8), band)], first_ref)
    copies.send(canvas.at[:, :, pl.ds(pl.multiple_of(far - low, 8), band)], second_ref)
    copies.send(canvas.at[:, :, band : band + mid_ref.shape[2]], mid_ref)
    for core in range(2):

        @pl.when(at_ref[0] == core)
        def _():
            pack_half(grads, core, keep_ref)
            pack_half(grads, 1 - core, send_ref)


def brightness(probe_ref):
    return jnp.sum(probe_ref[0] * probe_ref[0] + probe_ref[1] * probe_ref[1], axis=0)


def join_rows_kernel(
    copies, at_ref, obj_ref, row_a_ref, row_b_ref, tag_ref, tall_ref, col_a_ref, col_b_ref, tags_ref
):
    band = row_a_ref.shape[1] - 8
    size = obj_ref.shape[1]
    n = col_a_ref.shape[1]
    extent = tall_ref.shape[1]
    upper, lower = ordered(at_ref[5] == 1, row_a_ref[...], row_b_ref[...])
    tall_ref[:, :band] = upper[:, :band]
    tall_ref[:, band + size :] = lower[:, :band]
    tags_ref[...] = jnp.zeros_like(tags_ref)
    tags_ref[:1] = upper[0, band : band + 1, :n]
    tags_ref[1:2] = tag_ref[:1]
    tags_ref[2:3] = lower[0, band : band + 1, :n]
    copies.need(obj_ref)
    tall_ref[:, band : band + size] = obj_ref[...]
    lane = lax.broadcasted_iota(jnp.int32, (extent, n), 1)
    left = jnp.where(lane < band, tall_ref[0, :, :n], pltpu.roll(tall_ref[1, :, :n], band, 1))
    right = jnp.where(lane < band, pltpu.roll(tall_ref[0, :, size - n :], band, 1), tall_ref[1, :, size - n :])
    col_a_ref[:extent], col_b_ref[:extent] = ordered(at_ref[6] == 1, left, right)
    col_a_ref[extent:] = tags_ref[...]
    col_b_ref[extent:] = tags_ref[...]


def first_kernel(
    copies, off_ref, at_ref, tall_ref, col_a_ref, col_b_ref, probe_ref, meas_ref, fwd_ref, bwd_ref,
    first_ref, second_ref, mid_ref, keep_ref, send_ref, cells, bright_ref, canvas, grads,
):
    n = probe_ref.shape[2]
    half = n // 2
    extent = tall_ref.shape[1]
    lane = lax.broadcasted_iota(jnp.int32, (extent, n), 1)
    canvas[...] = jnp.zeros_like(canvas)
    bright_ref[...] = brightness(probe_ref)
    copies.ready(bright_ref)
    before, after = ordered(at_ref[6] == 1, col_a_ref[:extent], col_b_ref[:extent])
    strips = [
        (before, pltpu.roll(after, half, 1)),
        (pltpu.roll(before, half, 1), after),
    ]
    for ch in range(2):
        inner = [pltpu.roll(tall_ref[ch, :, k * n : (k + 1) * n], half, 1) for k in range(2)]
        row = [strips[ch][0], *inner, strips[ch][1]]
        for k in range(3):
            cells[ch, k] = jnp.where(lane < half, row[k], row[k + 1])
    copies.ready(cells)
    copies.need(fwd_ref, bwd_ref)
    sweep_positions(copies, off_ref, probe_ref, meas_ref, fwd_ref, bwd_ref, cells, canvas, grads)
    finish(copies, at_ref, canvas, grads, first_ref, second_ref, mid_ref, keep_ref, send_ref)


def light_peak(mine_ref, other_ref):
    best = [jnp.max(ref[pl.ds(DATA, PARTS, stride=CHUNK), :]) for ref in (mine_ref, other_ref)]
    return jnp.maximum(best[0], best[1])


def update_probes(at_ref, mine_ref, other_ref, probe_ref, grads, new_probe_ref):
    modes = probe_ref.shape[1]
    for core in range(2):

        @pl.when(at_ref[0] == core)
        def _():
            unpack_half(mine_ref, core, grads)
            unpack_half(other_ref, 1 - core, grads)

    density = grads[2 * modes]
    scale = 1.0 / (density + 0.1 * jnp.max(density))
    for part in range(2):
        for m in range(modes):
            old = probe_ref[part, m]
            new_probe_ref[part, m] = old + (grads[part * modes + m] - old * density) * scale


def updated(old, sums, light, peak):
    scale = 1.0 / (light + 0.1 * peak)
    return [old[ch] + (sums[ch] - old[ch] * light) * scale for ch in range(2)]


def next_kernel(
    copies, off_ref, at_ref, obj_ref, own_a_ref, own_b_ref, mid_ref, row_a_ref, row_b_ref, col_a_ref, col_b_ref, light_ref,
    mine_ref, other_ref, probe_ref, meas_ref, fwd_ref, bwd_ref,
    first_ref, second_ref, new_mid_ref, keep_ref, send_ref, new_obj_ref, bright_ref, new_probe_ref,
    canvas, grads,
):
    n = probe_ref.shape[2]
    blocks = obj_ref.shape[1]
    canvas[...] = jnp.zeros_like(canvas)
    peak = light_peak(mine_ref, other_ref)
    copies.need(probe_ref)
    update_probes(at_ref, mine_ref, other_ref, probe_ref, grads, new_probe_ref)
    copies.ready(new_probe_ref)
    bright_ref[...] = brightness(new_probe_ref)
    copies.ready(bright_ref)
    copies.need(obj_ref, own_a_ref, own_b_ref, mid_ref, row_a_ref, row_b_ref, col_a_ref, col_b_ref, light_ref)
    for j in range(3):
        rows = slice(j * n, (j + 1) * n)
        row = lax.broadcasted_iota(jnp.int32, (n, n), 0) + j * n
        row_ok = (row >= at_ref[1]) & (row < at_ref[2])
        for k in range(blocks):
            col = lax.broadcasted_iota(jnp.int32, (n, n), 1) + k * n
            inside = row_ok & (col >= at_ref[3]) & (col < at_ref[4])
            if j == 1:
                sums = mid_ref[:, k]
            else:
                ends = ordered(
                    at_ref[5] == 1, own_a_ref[:, k] + row_a_ref[:, k], own_b_ref[:, k] + row_b_ref[:, k]
                )
                sums = ends[j > 0]
            if k in (0, blocks - 1):
                sides = ordered(at_ref[6] == 1, col_a_ref[:, rows], col_b_ref[:, rows])
                sums = sums + sides[k > 0]
            new = updated(obj_ref[:, k, rows], sums, light_ref[k, rows], peak)
            for ch in range(2):
                new_obj_ref[ch, k, rows] = jnp.where(inside, new[ch], 0.0)
    copies.ready(new_obj_ref)
    copies.need(fwd_ref, bwd_ref)
    sweep_positions(copies, off_ref, new_probe_ref, meas_ref, fwd_ref, bwd_ref, new_obj_ref, canvas, grads)
    finish(copies, at_ref, canvas, grads, first_ref, second_ref, new_mid_ref, keep_ref, send_ref)


def last_kernel(
    copies, at_ref, obj_ref, sums_ref, col_a_ref, col_b_ref, light_ref, mine_ref, other_ref, probe_ref,
    out_ref, new_probe_ref, grads,
):
    n = probe_ref.shape[2]
    half = n // 2
    blocks = obj_ref.shape[1]
    tile = out_ref.shape[1]
    inner = slice(half, half + tile)
    copies.need(probe_ref)
    update_probes(at_ref, mine_ref, other_ref, probe_ref, grads, new_probe_ref)
    copies.ready(new_probe_ref)
    copies.need(obj_ref, sums_ref, col_a_ref, col_b_ref, light_ref)
    left, right = ordered(at_ref[6] == 1, col_a_ref[...], col_b_ref[...])
    peak = light_peak(mine_ref, other_ref)
    lane = lax.broadcasted_iota(jnp.int32, (tile, n), 1)
    rolled = []
    for k in range(blocks):
        sums = [sums_ref[ch, k] for ch in range(2)]
        if k == 0:
            sums[0] = sums[0] + jnp.where(lane < half, 0.0, left)
            sums[1] = sums[1] + jnp.where(lane < half, 0.0, pltpu.roll(left, half, 1))
        elif k == blocks - 1:
            sums[0] = sums[0] + jnp.where(lane < half, right, 0.0)
            sums[1] = sums[1] + jnp.where(lane < half, pltpu.roll(right, half, 1), 0.0)
        new = updated(obj_ref[:, k, inner], sums, light_ref[k, inner], peak)
        rolled.append([pltpu.roll(x, half, 1) for x in new])
    for k in range(blocks - 1):
        for ch in range(2):
            out_ref[ch, :, k * n : (k + 1) * n] = jnp.where(lane < half, rolled[k][ch], rolled[k + 1][ch])
    copies.ready(out_ref)


def fold_kernel(copies, at_ref, first_ref, second_ref, mid_ref, row_a_ref, row_b_ref, col_a_ref, col_b_ref):
    n = col_a_ref.shape[2]
    last = mid_ref.shape[1] - 1
    copies.need(first_ref, row_a_ref, second_ref, row_b_ref, mid_ref)
    sides = []
    for k in (0, last):
        top, low = ordered(
            at_ref[5] == 1, first_ref[:, k] + row_a_ref[:, k], second_ref[:, k] + row_b_ref[:, k]
        )
        sides.append((top, mid_ref[:, k], low))
    for j in range(3):
        rows = slice(j * n, (j + 1) * n)
        col_a_ref[:, rows], col_b_ref[:, rows] = ordered(at_ref[6] == 1, sides[0][j], sides[1][j])
    copies.ready(col_a_ref, col_b_ref)


def fold_inner_kernel(copies, at_ref, mid_ref, row_a_ref, row_b_ref, sums_ref, col_a_ref, col_b_ref):
    n = col_a_ref.shape[1]
    band = row_a_ref.shape[2]
    tile = mid_ref.shape[2]
    last = mid_ref.shape[1] - 1
    copies.need(mid_ref, row_a_ref, row_b_ref)
    upper, lower = ordered(at_ref[5] == 1, row_a_ref[...], row_b_ref[...])
    sums_ref[:, :, :band] = mid_ref[:, :, :band] + upper
    sums_ref[:, :, band : tile - band] = mid_ref[:, :, band : tile - band]
    sums_ref[:, :, tile - band :] = mid_ref[:, :, tile - band :] + lower
    lane = lax.broadcasted_iota(jnp.int32, (tile, n), 1)
    left = jnp.where(lane < band, sums_ref[0, 0], pltpu.roll(sums_ref[1, 0], band, 1))
    right = jnp.where(lane < band, pltpu.roll(sums_ref[1, last], band, 1), sums_ref[0, last])
    col_a_ref[...], col_b_ref[...] = ordered(at_ref[6] == 1, left, right)
    copies.ready(col_a_ref, col_b_ref, sums_ref)


def place_lights(tag_ref, bright_ref, canvas, spots, rim, tile):
    n = bright_ref.shape[1]
    half = n // 2
    group = 4
    lane = lax.broadcasted_iota(jnp.int32, (n, n), 1)
    count = jnp.int32(0)
    for t in range(9):
        if rim and t == 4:
            continue
        down, across = t % 3 - 1, t // 3 - 1

        def gather(p, count):
            u = tag_ref[t, 2 * p]
            v = tag_ref[t, 2 * p + 1]
            held = u > 0
            u = u + (n - 1 + down * tile)
            v = v + (n - 1 + across * tile)
            inner = (u > half) & (u < tile + n + half) & (v > half) & (v < tile + n + half)
            if rim:
                held = held & ~inner & (u > 0) & (u < tile + 2 * n) & (v > 0) & (v < tile + 2 * n)
            else:
                held = held & inner
            spots[count, 0] = u
            spots[count, 1] = v
            return count + held.astype(jnp.int32)

        count = lax.fori_loop(0, tag_ref.shape[1] // 2, gather, count, unroll=16)
    for j in range(group):
        spots[count + j, 0] = 0
        spots[count + j, 1] = 0
    canvas[...] = jnp.zeros_like(canvas)
    value = bright_ref[...]

    def step(i, carry):
        held = []
        for j in range(group):
            u = spots[i * group + j, 0]
            v = spots[i * group + j, 1]
            s = lax.rem(v, n)
            held.append((u, v // n, s, pltpu.roll(value, s, 1)))
        for u, k, s, rolled in held:
            canvas[k, pl.ds(u, n), :] += jnp.where(lane >= s, rolled, 0.0)
            canvas[k + 1, pl.ds(u, n), :] += jnp.where(lane >= s, 0.0, rolled)
        return carry

    lax.fori_loop(0, (count + group - 1) // group, step, 0)


def light_kernel(copies, tag_ref, bright_ref, light_ref, peak_ref, canvas, spots):
    n = bright_ref.shape[1]
    half = n // 2
    blocks, extent = light_ref.shape[:2]
    copies.need(bright_ref)
    place_lights(tag_ref, bright_ref, canvas, spots, False, extent - n)
    light_ref[...] = canvas[1 : 1 + blocks, n : n + extent]
    copies.ready(light_ref)
    lane = lax.broadcasted_iota(jnp.int32, (extent - n, n), 1)
    best = None
    for k in range(blocks):
        mine = light_ref[k, half : extent - half]
        if k == 0:
            mine = jnp.where(lane >= half, mine, 0.0)
        elif k == blocks - 1:
            mine = jnp.where(lane < half, mine, 0.0)
        best = mine if best is None else jnp.maximum(best, mine)
    peak_ref[...] = jnp.full(peak_ref.shape, jnp.max(best), F32)


def more_light_kernel(copies, tag_ref, bright_ref, light_ref, all_ref, canvas, spots):
    n = bright_ref.shape[1]
    blocks, extent = light_ref.shape[:2]
    copies.need(bright_ref)
    place_lights(tag_ref, bright_ref, canvas, spots, True, extent - n)
    copies.need(light_ref)
    all_ref[...] = light_ref[...] + canvas[1 : 1 + blocks, n : n + extent]
    copies.ready(all_ref)


def share_kernel(copies, parts_ref, peak_ref, out_ref):
    share = parts_ref[:CHUNK]
    for s in range(1, PARTS):
        share = share + parts_ref[s * CHUNK : (s + 1) * CHUNK]
    row = lax.broadcasted_iota(jnp.int32, share.shape, 0)
    out_ref[...] = jnp.where(row < DATA, share, peak_ref[:1])


class Far:
    def __init__(self, value, parts=1):
        self.value = value
        self.parts = parts


class Raw(Far):
    pass


class Copies:
    def __init__(self):
        self.ins = {}
        self.outs = {}
        self.sems = {}
        self.sent = []

    def need(self, *refs):
        for ref in refs:
            copy = self.ins.pop(id(ref), None)
            if copy is not None:
                copy(0).wait()

    def need_part(self, ref, i):
        if id(ref) in self.ins:
            self.ins[id(ref)](i).wait()

    def ready(self, *refs):
        for ref in refs:
            copy = self.outs.get(id(ref))
            if copy is not None:
                copy.start()
                self.sent.append(copy)

    def send(self, local, remote):
        copy = pltpu.make_async_copy(local, remote, self.sems[id(remote)])
        copy.start()
        self.sent.append(copy)


def part_copy(remote, local, sems, first, parts):
    size = local.shape[0] // parts

    def copy(i):
        rows = pl.ds(i * size, size)
        return pltpu.make_async_copy(remote.at[rows], local.at[rows], sems.at[first + i])

    return copy


def call(kernel, outs, scratch, args, scalars, name, limit=24):
    info = list(args) + list(outs)
    split = len(args)
    values = [x.value if isinstance(x, Far) else x for x in info]
    far = [isinstance(x, Far) for x in info]
    raw = [isinstance(x, Raw) for x in info]
    buffers, sem_at, count = [], {}, 0
    for i, value in enumerate(values):
        if far[i]:
            sem_at[i] = count
            count += info[i].parts
            if not raw[i]:
                buffers.append(pltpu.VMEM(value.shape, value.dtype) if i < split else pltpu.VMEM(value, F32))

    def whole(*refs):
        sems = refs[-1]
        refs = list(refs[:-1])
        spare = iter(refs[len(info) : len(info) + len(buffers)])
        rest = refs[len(info) + len(buffers) :]
        copies = Copies()
        for i in sem_at:
            first = sem_at[i]
            if raw[i]:
                copies.sems[id(refs[i])] = sems.at[first]
                continue
            remote, local = refs[i], next(spare)
            refs[i] = local
            if i < split:
                copies.ins[id(local)] = part_copy(remote, local, sems, first, info[i].parts)
                for j in range(info[i].parts):
                    copies.ins[id(local)](j).start()
            else:
                copies.outs[id(local)] = pltpu.make_async_copy(local, remote, sems.at[first])
        kernel(copies, *refs[: len(info)], *rest)
        for copy in copies.sent:
            copy.wait()

    far_spec = pl.BlockSpec(memory_space=pltpu.HBM)
    specs = [SM if i < scalars else (far_spec if far[i] else VM) for i in range(len(info))]
    operands = [
        pltpu.with_memory_space_constraint(x, pltpu.HBM) if is_far else x for x, is_far in zip(values[:split], far)
    ]
    return pl.pallas_call(
        whole,
        out_shape=tuple(
            pltpu.HBM(x, F32) if is_far else jax.ShapeDtypeStruct(x, F32) for x, is_far in zip(values[split:], far[split:])
        ),
        in_specs=specs[:split],
        out_specs=tuple(specs[split:]),
        scratch_shapes=buffers
        + [x if x is SPOTS else pltpu.VMEM(x, F32) for x in scratch]
        + [pltpu.SemaphoreType.DMA((max(count, 1),))],
        compiler_params=pltpu.CompilerParams(vmem_limit_bytes=limit * 1024 * 1024),
        name=name,
    )(*operands)


def length(axes):
    return functools.reduce(lambda a, b: a * b, [lax.axis_size(axis) for axis in axes])


def exchange(first, second, axes):
    count = length(axes)
    first = lax.ppermute(first, axes, [(i, i ^ 1) for i in range(count)])
    pairs = [(i, i + 1) for i in range(1, count - 1, 2)]
    second = lax.ppermute(second, axes, pairs + [(j, i) for i, j in pairs])
    return first, second


def swap(value, axes):
    count = length(axes)
    return lax.ppermute(value, axes, [(i, count - 1 - i) for i in range(count)])


def share_over_x(share):
    near = swap(share, ("xl",))
    far = swap(share, ("xh",))
    cross = swap(share, ("xh", "xl"))
    at = lax.broadcasted_iota(jnp.int32, share.shape, 0)
    added = (share + near) + (far + cross)
    largest = jnp.maximum(jnp.maximum(share, near), jnp.maximum(far, cross))
    return jnp.where(at < DATA, added, largest)


def body(object_field, probe_modes, scan_offsets, measured):
    n = probe_modes.shape[-1]
    modes = probe_modes.shape[1]
    half = n // 2
    tile = object_field.shape[1]
    extent = tile + n
    blocks = extent // n
    positions = scan_offsets.shape[2]
    offsets = scan_offsets.reshape(positions, 2)
    amplitudes = measured.reshape(positions, n, n)
    tables = dft_pair(n)
    row = lax.axis_index(ROW)
    col = lax.axis_index(COL)
    info = jnp.stack(
        [
            lax.axis_index("core"),
            jnp.where(row == 0, half, 0),
            jnp.where(row == length(ROW) - 1, extent - half, extent),
            jnp.where(col == 0, half, 0),
            jnp.where(col == length(COL) - 1, extent - half, extent),
            row % 2,
            col % 2,
        ]
    ).astype(jnp.int32)

    tag = (offsets + 1).astype(F32).reshape(1, 2 * positions)
    tag_rows = jnp.pad(tag, ((0, 7), (0, n - 2 * positions)))
    tag_block = jnp.pad(tag[None], ((0, 1), (0, 7), (0, tile - 2 * positions)))
    low = (1 - row % 2) * (tile - half)
    first = lax.dynamic_slice_in_dim(object_field, low, half, 1)
    second = lax.dynamic_slice_in_dim(object_field, tile - half - low, half, 1)
    row_a, row_b = exchange(*(jnp.concatenate([x, tag_block], 1) for x in (first, second)), ROW)
    strip = (extent + 8, n)
    tall, col_a, col_b, own = call(
        join_rows_kernel,
        [(2, extent, tile), strip, strip, (8, n)],
        [],
        [info, Far(object_field), row_a, row_b, tag_rows],
        1,
        "join_rows",
    )
    col_a, col_b = exchange(col_a, col_b, COL)
    odd = col % 2 == 1
    before, after = ordered(odd, col_a[extent : extent + 3, :32], col_b[extent : extent + 3, :32])
    tags = jnp.concatenate([before, own[:3, :32], after], 0)
    tags = tags.astype(jnp.int32)

    cells = (2, blocks, extent, n)
    canvas = (blocks + 2, extent + 2 * n, n)
    lights = (blocks, extent, n)
    grads = (2 * modes + 1, n, n)
    packed = (PARTS * CHUNK, n)
    band = (2, blocks, n, n)
    probes = probe_modes
    tables = [Far(x) for x in tables]
    amplitudes = Far(amplitudes, positions // BATCH)
    for sweep in range(ITERS):
        last = sweep == ITERS - 1
        bands = [(2, blocks, x, n) for x in ((half, half, tile) if last else (n, n, n))]
        outs = [Raw(x) for x in bands] + [packed, packed, Far(cells), Far((n, n))]
        if sweep == 0:
            args = [offsets, info, tall, col_a, col_b, probes, amplitudes, *tables]
            first, second, mid, keep, send, cells_now, bright = call(first_kernel, outs, [cells, grads], args, 2, "first_sweep")
        else:
            held = [Far(x) for x in (cells_now, *sums, light)]
            args = [offsets, info, *held, mine, other, Far(probes), amplitudes, *tables]
            first, second, mid, keep, send, cells_now, bright, probes = call(
                next_kernel, outs + [Far(probes.shape)], [cells, grads], args, 2, "next_sweep"
            )
        received = swap(send, ("core",))
        received, first, second, bright = lax.optimization_barrier((received, first, second, bright))
        parts = lax.all_to_all(keep + received, RING, 0, 0, tiled=True)
        light, peak = call(light_kernel, [Far(lights), (8, n)], [canvas, SPOTS], [tags, Far(bright)], 1, "light")
        row_a, row_b = exchange(first, second, ROW)
        if last:
            parts, row_a, row_b = lax.optimization_barrier((parts, row_a, row_b))
        else:
            parts, row_a = lax.optimization_barrier((parts, row_a))
        share = call(share_kernel, [(CHUNK, n)], [], [parts, peak], 0, "share")[0]
        share = share_over_x(share)
        copies = jnp.broadcast_to(share[None], (PARTS,) + share.shape).reshape(packed)
        light, copies, row_b = lax.optimization_barrier((light, copies, row_b))
        mine = lax.all_to_all(copies, RING, 0, 0, tiled=True)
        if last:
            outs = [Far((2, blocks, tile, n)), Far((tile, n)), Far((tile, n))]
            args = [info] + [Far(x) for x in (mid, row_a, row_b)]
            sums, col_a, col_b = call(fold_inner_kernel, outs, [], args, 1, "fold_inner")
            sums = [sums]
        else:
            side = (2, extent, n)
            outs = [Far(side), Far(side)]
            args = [info] + [Far(x) for x in (first, second, mid, row_a, row_b)]
            col_a, col_b = call(fold_kernel, outs, [], args, 1, "fold_rows")
            sums = [first, second, mid, row_a, row_b]
            args = [tags, Far(bright), Far(light)]
            light = call(more_light_kernel, [Far(lights)], [canvas, SPOTS], args, 1, "more_light")[0]
        col_a, col_b = exchange(col_a, col_b, COL)
        mine, col_a, col_b, light = lax.optimization_barrier((mine, col_a, col_b, light))
        sums += [col_a, col_b]
        other = swap(mine, ("core",))
    held = [Far(x) for x in (cells_now, *sums, light)]
    args = [info, *held, mine, other, Far(probes)]
    return call(last_kernel, [Far(object_field.shape), Far(probes.shape)], [grads], args, 1, "last_update")


def solution(mesh):
    names = tuple(name for name, _ in SPLIT)
    sizes = tuple(size for _, size in SPLIT)
    fine = Mesh(mesh.devices.reshape(sizes), names)
    return jax.shard_map(
        body,
        mesh=fine,
        in_specs=(
            P(None, ROW, COL),
            P(),
            P(ROW, COL, None, None),
            P(ROW, COL, None, None, None),
        ),
        out_specs=(P(None, ROW, COL), P()),
        check_vma=False,
    )
```

```python
import functools

import jax
import jax.numpy as jnp
import numpy as np
from jax import lax
from jax.experimental import pallas as pl
from jax.experimental.pallas import tpu as pltpu
from jax.sharding import Mesh, PartitionSpec as P

ITERS = 2
BATCH = 4
SPLIT = (("y", 4), ("xh", 2), ("core", 2), ("xl", 2), ("z", 8))
ROW = ("y", "xh", "core")
COL = ("xl", "z")
RING = ("y", "z")
PARTS = 32
CHUNK = 24
DATA = 18

VM = pl.BlockSpec(memory_space=pltpu.VMEM)
SM = pl.BlockSpec(memory_space=pltpu.SMEM)
F32 = jnp.float32
SPOTS = pltpu.SMEM((9 * 16 + 4, 2), jnp.int32)


def dft_pair(n):
    index = np.arange(n)
    angle = (index[:, None] * index[None, :] % n) * (2.0 * np.pi / n)
    c = np.cos(angle) / np.sqrt(n)
    s = np.sin(angle) / np.sqrt(n)
    forward = np.block([[c, s], [-s, c]])
    backward = np.block([[c, -s], [s, c]])
    return jnp.asarray(forward, jnp.bfloat16), jnp.asarray(backward, jnp.bfloat16)


def ordered(odd, first, second):
    return jnp.where(odd, first, second), jnp.where(odd, second, first)


def total(values):
    return functools.reduce(jnp.add, values)


def place(canvas, ch, where, lane, value):
    u, k, s = where
    n = value.shape[0]
    rolled = pltpu.roll(value, s, 1)
    canvas[ch, k, pl.ds(u, n), :] += jnp.where(lane >= s, rolled, 0.0)
    canvas[ch, k + 1, pl.ds(u, n), :] += jnp.where(lane >= s, 0.0, rolled)


def sweep_positions(copies, off_ref, probe_ref, meas_ref, fwd_ref, bwd_ref, cells, canvas, grads):
    modes = probe_ref.shape[1]
    n = probe_ref.shape[2]
    grads[...] = jnp.zeros_like(grads)
    lane = lax.broadcasted_iota(jnp.int32, (n, n), 1)

    def window(ch, where):
        u, k, s = where
        left = cells[ch, k, pl.ds(u, n), :]
        right = cells[ch, k + 1, pl.ds(u, n), :]
        return pltpu.roll(jnp.where(lane >= s, left, right), n - s, 1)

    def transform(field, left, right):
        sec = jnp.dot(left, field, preferred_element_type=F32).astype(jnp.bfloat16)
        parts = [slice(m * n, (m + 1) * n) for m in range(modes)]
        rows = [jnp.concatenate([sec[:n, part], sec[n:, part]], 1) for part in parts]
        return jnp.dot(jnp.concatenate(rows, 0), right, preferred_element_type=F32)

    def paired(re_parts, im_parts):
        re_all = jnp.concatenate([x.astype(jnp.bfloat16) for x in re_parts], 1)
        im_all = jnp.concatenate([x.astype(jnp.bfloat16) for x in im_parts], 1)
        return jnp.concatenate([re_all, im_all], 0)

    def split(wave):
        return [(wave[m * n : (m + 1) * n, :n], wave[m * n : (m + 1) * n, n:]) for m in range(modes)]

    def spot(q):
        u = off_ref[q, 0]
        v = off_ref[q, 1]
        return u, v // n, lax.rem(v, n)

    def step(i, carry):
        copies.need_part(meas_ref, i)
        probes = [(probe_ref[0, m], probe_ref[1, m]) for m in range(modes)]
        spots = [spot(i * BATCH + j) for j in range(BATCH)]
        wins = [(window(0, where), window(1, where)) for where in spots]
        exits = []
        for w_re, w_im in wins:
            re_parts = [p_re * w_re - p_im * w_im for p_re, p_im in probes]
            im_parts = [p_re * w_im + p_im * w_re for p_re, p_im in probes]
            exits.append(paired(re_parts, im_parts))
        fars = [split(transform(x, fwd_ref[...], bwd_ref[...])) for x in exits]
        corrected = []
        for j, far in enumerate(fars):
            power = total([re * re + im * im for re, im in far])
            raised = power + 1.0
            root = lax.rsqrt(raised)
            root = root * (1.5 - 0.5 * raised * root * root)
            scale = meas_ref[i * BATCH + j] * root
            corrected.append(paired([re * scale for re, _ in far], [im * scale for _, im in far]))
        backs = [split(transform(x, bwd_ref[...], fwd_ref[...])) for x in corrected]
        for where, back in zip(spots, backs):
            place(canvas, 0, where, lane, total([p[0] * b[0] + p[1] * b[1] for p, b in zip(probes, back)]))
            place(canvas, 1, where, lane, total([p[0] * b[1] - p[1] * b[0] for p, b in zip(probes, back)]))
        for m in range(modes):
            pairs = [(w, back[m]) for w, back in zip(wins, backs)]
            grads[m] += total([w[0] * b[0] + w[1] * b[1] for w, b in pairs])
            grads[modes + m] += total([w[0] * b[1] - w[1] * b[0] for w, b in pairs])
        grads[2 * modes] += total([w[0] * w[0] + w[1] * w[1] for w in wins])
        return carry

    lax.fori_loop(0, meas_ref.shape[0] // BATCH, step, 0)


def pack_half(grads, half, out_ref):
    planes = grads.shape[0]
    out_ref[...] = jnp.zeros_like(out_ref)
    for c in range(planes):
        for t in range(2):
            out_ref[pl.ds(2 * c + t, PARTS, stride=CHUNK), :] = grads[
                c, pl.ds(half * 2 * PARTS + t, PARTS, stride=2), :
            ]


def unpack_half(in_ref, half, grads):
    planes = grads.shape[0]
    for c in range(planes):
        for t in range(2):
            grads[c, pl.ds(half * 2 * PARTS + t, PARTS, stride=2), :] = in_ref[
                pl.ds(2 * c + t, PARTS, stride=CHUNK), :
            ]


def finish(copies, at_ref, canvas, grads, first_ref, second_ref, mid_ref, keep_ref, send_ref):
    band = first_ref.shape[2]
    far = canvas.shape[2] - band
    low = (1 - at_ref[5]) * far
    copies.send(canvas.at[:, :, pl.ds(pl.multiple_of(low, 8), band)], first_ref)
    copies.send(canvas.at[:, :, pl.ds(pl.multiple_of(far - low, 8), band)], second_ref)
    copies.send(canvas.at[:, :, band : band + mid_ref.shape[2]], mid_ref)
    for core in range(2):

        @pl.when(at_ref[0] == core)
        def _():
            pack_half(grads, core, keep_ref)
            pack_half(grads, 1 - core, send_ref)


def brightness(probe_ref):
    return jnp.sum(probe_ref[0] * probe_ref[0] + probe_ref[1] * probe_ref[1], axis=0)


def side_by_side(cells, lane):
    n = lane.shape[1]
    half = n // 2
    size = cells.shape[2]
    left = jnp.where(lane < half, cells[0, :, :n], pltpu.roll(cells[1, :, :n], half, 1))
    right = jnp.where(lane < half, pltpu.roll(cells[0, :, size - n :], half, 1), cells[1, :, size - n :])
    return left, right


def pack_kernel(copies, at_ref, obj_ref, tag_ref, row_a_ref, row_b_ref, col_a_ref, col_b_ref):
    size = obj_ref.shape[1]
    n = col_a_ref.shape[1]
    half = n // 2
    copies.need(obj_ref)
    row_a_ref[:, :half], row_b_ref[:, :half] = ordered(at_ref[5] == 1, obj_ref[:, :half], obj_ref[:, size - half :])
    for ref in (row_a_ref, row_b_ref):
        ref[:, half:] = jnp.zeros((2, 8, size), F32)
        ref[0, half:, :n] = tag_ref[...]
    lane = lax.broadcasted_iota(jnp.int32, (size, n), 1)
    left, right = side_by_side(obj_ref[...], lane)
    col_a_ref[:size], col_b_ref[:size] = ordered(at_ref[6] == 1, left, right)
    col_a_ref[size:] = tag_ref[...]
    col_b_ref[size:] = tag_ref[...]


def corner_kernel(copies, at_ref, row_a_ref, row_b_ref, end_a_ref, end_b_ref):
    n = end_a_ref.shape[1]
    half = n // 2
    lane = lax.broadcasted_iota(jnp.int32, (half, n), 1)
    rows = ordered(at_ref[5] == 1, row_a_ref[...], row_b_ref[...])
    for j, strip in enumerate(rows):
        left, right = side_by_side(strip[:, :half], lane)
        part = slice(j * half, (j + 1) * half)
        end_a_ref[part], end_b_ref[part] = ordered(at_ref[6] == 1, left, right)
    for ref in (end_a_ref, end_b_ref):
        ref[n:] = jnp.zeros((8, n), F32)
        for j, strip in enumerate(rows):
            ref[n + j : n + j + 1] = strip[0, half : half + 1, :n]


def first_kernel(
    copies, off_ref, at_ref, obj_ref, tag_ref,
    row_a_ref, row_b_ref, col_a_ref, col_b_ref, end_a_ref, end_b_ref,
    probe_ref, meas_ref, fwd_ref, bwd_ref,
    first_ref, second_ref, mid_ref, keep_ref, send_ref, cells, bright_ref, tags_ref, canvas, grads,
):
    n = probe_ref.shape[2]
    half = n // 2
    size = obj_ref.shape[1]
    odd_row = at_ref[5] == 1
    odd_col = at_ref[6] == 1
    canvas[...] = jnp.zeros_like(canvas)
    bright_ref[...] = brightness(probe_ref)
    copies.ready(bright_ref)
    upper, lower = ordered(odd_row, row_a_ref[...], row_b_ref[...])
    before, after = ordered(odd_col, col_a_ref[...], col_b_ref[...])
    ends = ordered(odd_col, end_a_ref[...], end_b_ref[...])
    over = [x[:half] for x in ends]
    under = [x[half:n] for x in ends]
    tags_ref[...] = jnp.zeros_like(tags_ref)
    tags_ref[:9] = jnp.concatenate(
        [
            ends[0][n : n + 1], before[size : size + 1], ends[0][n + 1 : n + 2],
            upper[0, half : half + 1, :n], tag_ref[:1], lower[0, half : half + 1, :n],
            ends[1][n : n + 1], after[size : size + 1], ends[1][n + 1 : n + 2],
        ],
        0,
    )
    copies.need(obj_ref)
    bands = (
        (0, half, upper[:, :half], over[0], over[1]),
        (half, size, obj_ref[...], before[:size], after[:size]),
        (half + size, half, lower[:, :half], under[0], under[1]),
    )
    for start, count, centre, left, right in bands:
        rows = slice(start, start + count)
        lane = lax.broadcasted_iota(jnp.int32, (count, n), 1)
        strips = [(left, pltpu.roll(right, half, 1)), (pltpu.roll(left, half, 1), right)]
        for ch in range(2):
            inner = [pltpu.roll(centre[ch, :, k * n : (k + 1) * n], half, 1) for k in range(2)]
            row = [strips[ch][0], *inner, strips[ch][1]]
            for k in range(3):
                cells[ch, k, rows] = jnp.where(lane < half, row[k], row[k + 1])
    copies.ready(cells)
    copies.need(fwd_ref, bwd_ref)
    sweep_positions(copies, off_ref, probe_ref, meas_ref, fwd_ref, bwd_ref, cells, canvas, grads)
    finish(copies, at_ref, canvas, grads, first_ref, second_ref, mid_ref, keep_ref, send_ref)


def light_peak(mine_ref, other_ref):
    best = [jnp.max(ref[pl.ds(DATA, PARTS, stride=CHUNK), :]) for ref in (mine_ref, other_ref)]
    return jnp.maximum(best[0], best[1])


def update_probes(at_ref, mine_ref, other_ref, probe_ref, grads, new_probe_ref):
    modes = probe_ref.shape[1]
    for core in range(2):

        @pl.when(at_ref[0] == core)
        def _():
            unpack_half(mine_ref, core, grads)
            unpack_half(other_ref, 1 - core, grads)

    density = grads[2 * modes]
    scale = 1.0 / (density + 0.1 * jnp.max(density))
    for part in range(2):
        for m in range(modes):
            old = probe_ref[part, m]
            new_probe_ref[part, m] = old + (grads[part * modes + m] - old * density) * scale


def updated(old, sums, light, peak):
    scale = 1.0 / (light + 0.1 * peak)
    return [old[ch] + (sums[ch] - old[ch] * light) * scale for ch in range(2)]


def next_kernel(
    copies, off_ref, at_ref, obj_ref, own_a_ref, own_b_ref, mid_ref, row_a_ref, row_b_ref, col_a_ref, col_b_ref, light_ref,
    mine_ref, other_ref, probe_ref, meas_ref, fwd_ref, bwd_ref,
    first_ref, second_ref, new_mid_ref, keep_ref, send_ref, new_obj_ref, bright_ref, new_probe_ref,
    canvas, grads,
):
    n = probe_ref.shape[2]
    blocks = obj_ref.shape[1]
    canvas[...] = jnp.zeros_like(canvas)
    peak = light_peak(mine_ref, other_ref)
    copies.need(probe_ref)
    update_probes(at_ref, mine_ref, other_ref, probe_ref, grads, new_probe_ref)
    copies.ready(new_probe_ref)
    bright_ref[...] = brightness(new_probe_ref)
    copies.ready(bright_ref)
    copies.need(obj_ref, own_a_ref, own_b_ref, mid_ref, row_a_ref, row_b_ref, col_a_ref, col_b_ref, light_ref)
    for j in range(3):
        rows = slice(j * n, (j + 1) * n)
        row = lax.broadcasted_iota(jnp.int32, (n, n), 0) + j * n
        row_ok = (row >= at_ref[1]) & (row < at_ref[2])
        for k in range(blocks):
            col = lax.broadcasted_iota(jnp.int32, (n, n), 1) + k * n
            inside = row_ok & (col >= at_ref[3]) & (col < at_ref[4])
            if j == 1:
                sums = mid_ref[:, k]
            else:
                ends = ordered(
                    at_ref[5] == 1, own_a_ref[:, k] + row_a_ref[:, k], own_b_ref[:, k] + row_b_ref[:, k]
                )
                sums = ends[j > 0]
            if k in (0, blocks - 1):
                sides = ordered(at_ref[6] == 1, col_a_ref[:, rows], col_b_ref[:, rows])
                sums = sums + sides[k > 0]
            new = updated(obj_ref[:, k, rows], sums, light_ref[k, rows], peak)
            for ch in range(2):
                new_obj_ref[ch, k, rows] = jnp.where(inside, new[ch], 0.0)
    copies.ready(new_obj_ref)
    copies.need(fwd_ref, bwd_ref)
    sweep_positions(copies, off_ref, new_probe_ref, meas_ref, fwd_ref, bwd_ref, new_obj_ref, canvas, grads)
    finish(copies, at_ref, canvas, grads, first_ref, second_ref, new_mid_ref, keep_ref, send_ref)


def last_kernel(
    copies, at_ref, obj_ref, sums_ref, col_a_ref, col_b_ref, light_ref, mine_ref, other_ref, probe_ref,
    out_ref, new_probe_ref, grads,
):
    n = probe_ref.shape[2]
    half = n // 2
    blocks = obj_ref.shape[1]
    tile = out_ref.shape[1]
    inner = slice(half, half + tile)
    copies.need(probe_ref)
    update_probes(at_ref, mine_ref, other_ref, probe_ref, grads, new_probe_ref)
    copies.ready(new_probe_ref)
    copies.need(obj_ref, sums_ref, col_a_ref, col_b_ref, light_ref)
    left, right = ordered(at_ref[6] == 1, col_a_ref[...], col_b_ref[...])
    peak = light_peak(mine_ref, other_ref)
    lane = lax.broadcasted_iota(jnp.int32, (tile, n), 1)
    rolled = []
    for k in range(blocks):
        sums = [sums_ref[ch, k] for ch in range(2)]
        if k == 0:
            sums[0] = sums[0] + jnp.where(lane < half, 0.0, left)
            sums[1] = sums[1] + jnp.where(lane < half, 0.0, pltpu.roll(left, half, 1))
        elif k == blocks - 1:
            sums[0] = sums[0] + jnp.where(lane < half, right, 0.0)
            sums[1] = sums[1] + jnp.where(lane < half, pltpu.roll(right, half, 1), 0.0)
        new = updated(obj_ref[:, k, inner], sums, light_ref[k, inner], peak)
        rolled.append([pltpu.roll(x, half, 1) for x in new])
    for k in range(blocks - 1):
        for ch in range(2):
            out_ref[ch, :, k * n : (k + 1) * n] = jnp.where(lane < half, rolled[k][ch], rolled[k + 1][ch])
    copies.ready(out_ref)


def fold_kernel(copies, at_ref, first_ref, second_ref, mid_ref, row_a_ref, row_b_ref, col_a_ref, col_b_ref):
    n = col_a_ref.shape[2]
    last = mid_ref.shape[1] - 1
    copies.need(first_ref, row_a_ref, second_ref, row_b_ref, mid_ref)
    sides = []
    for k in (0, last):
        top, low = ordered(
            at_ref[5] == 1, first_ref[:, k] + row_a_ref[:, k], second_ref[:, k] + row_b_ref[:, k]
        )
        sides.append((top, mid_ref[:, k], low))
    for j in range(3):
        rows = slice(j * n, (j + 1) * n)
        col_a_ref[:, rows], col_b_ref[:, rows] = ordered(at_ref[6] == 1, sides[0][j], sides[1][j])
    copies.ready(col_a_ref, col_b_ref)


def fold_inner_kernel(copies, at_ref, mid_ref, row_a_ref, row_b_ref, sums_ref, col_a_ref, col_b_ref):
    n = col_a_ref.shape[1]
    band = row_a_ref.shape[2]
    tile = mid_ref.shape[2]
    last = mid_ref.shape[1] - 1
    copies.need(mid_ref, row_a_ref, row_b_ref)
    upper, lower = ordered(at_ref[5] == 1, row_a_ref[...], row_b_ref[...])
    sums_ref[:, :, :band] = mid_ref[:, :, :band] + upper
    sums_ref[:, :, band : tile - band] = mid_ref[:, :, band : tile - band]
    sums_ref[:, :, tile - band :] = mid_ref[:, :, tile - band :] + lower
    lane = lax.broadcasted_iota(jnp.int32, (tile, n), 1)
    left = jnp.where(lane < band, sums_ref[0, 0], pltpu.roll(sums_ref[1, 0], band, 1))
    right = jnp.where(lane < band, pltpu.roll(sums_ref[1, last], band, 1), sums_ref[0, last])
    col_a_ref[...], col_b_ref[...] = ordered(at_ref[6] == 1, left, right)
    copies.ready(col_a_ref, col_b_ref, sums_ref)


def place_lights(tag_ref, bright_ref, canvas, spots, rim, tile):
    n = bright_ref.shape[1]
    half = n // 2
    group = 4
    lane = lax.broadcasted_iota(jnp.int32, (n, n), 1)
    count = jnp.int32(0)
    for t in range(9):
        if rim and t == 4:
            continue
        down, across = t % 3 - 1, t // 3 - 1

        def gather(p, count):
            u = tag_ref[t, 2 * p]
            v = tag_ref[t, 2 * p + 1]
            held = u > 0
            u = u + (n - 1 + down * tile)
            v = v + (n - 1 + across * tile)
            inner = (u > half) & (u < tile + n + half) & (v > half) & (v < tile + n + half)
            if rim:
                held = held & ~inner & (u > 0) & (u < tile + 2 * n) & (v > 0) & (v < tile + 2 * n)
            else:
                held = held & inner
            spots[count, 0] = u
            spots[count, 1] = v
            return count + held.astype(jnp.int32)

        count = lax.fori_loop(0, tag_ref.shape[1] // 2, gather, count, unroll=16)
    for j in range(group):
        spots[count + j, 0] = 0
        spots[count + j, 1] = 0
    canvas[...] = jnp.zeros_like(canvas)
    value = bright_ref[...]

    def step(i, carry):
        held = []
        for j in range(group):
            u = spots[i * group + j, 0]
            v = spots[i * group + j, 1]
            s = lax.rem(v, n)
            held.append((u, v // n, s, pltpu.roll(value, s, 1)))
        for u, k, s, rolled in held:
            canvas[k, pl.ds(u, n), :] += jnp.where(lane >= s, rolled, 0.0)
            canvas[k + 1, pl.ds(u, n), :] += jnp.where(lane >= s, 0.0, rolled)
        return carry

    lax.fori_loop(0, (count + group - 1) // group, step, 0)


def light_kernel(copies, tag_ref, bright_ref, light_ref, peak_ref, canvas, spots):
    n = bright_ref.shape[1]
    half = n // 2
    blocks, extent = light_ref.shape[:2]
    copies.need(bright_ref)
    place_lights(tag_ref, bright_ref, canvas, spots, False, extent - n)
    light_ref[...] = canvas[1 : 1 + blocks, n : n + extent]
    copies.ready(light_ref)
    lane = lax.broadcasted_iota(jnp.int32, (extent - n, n), 1)
    best = None
    for k in range(blocks):
        mine = light_ref[k, half : extent - half]
        if k == 0:
            mine = jnp.where(lane >= half, mine, 0.0)
        elif k == blocks - 1:
            mine = jnp.where(lane < half, mine, 0.0)
        best = mine if best is None else jnp.maximum(best, mine)
    peak_ref[...] = jnp.full(peak_ref.shape, jnp.max(best), F32)


def more_light_kernel(copies, tag_ref, bright_ref, light_ref, all_ref, canvas, spots):
    n = bright_ref.shape[1]
    blocks, extent = light_ref.shape[:2]
    copies.need(bright_ref)
    place_lights(tag_ref, bright_ref, canvas, spots, True, extent - n)
    copies.need(light_ref)
    all_ref[...] = light_ref[...] + canvas[1 : 1 + blocks, n : n + extent]
    copies.ready(all_ref)


def share_kernel(copies, parts_ref, peak_ref, out_ref):
    share = parts_ref[:CHUNK]
    for s in range(1, PARTS):
        share = share + parts_ref[s * CHUNK : (s + 1) * CHUNK]
    row = lax.broadcasted_iota(jnp.int32, share.shape, 0)
    out_ref[...] = jnp.where(row < DATA, share, peak_ref[:1])


class Far:
    def __init__(self, value, parts=1):
        self.value = value
        self.parts = parts


class Raw(Far):
    pass


class Copies:
    def __init__(self):
        self.ins = {}
        self.outs = {}
        self.sems = {}
        self.sent = []

    def need(self, *refs):
        for ref in refs:
            copy = self.ins.pop(id(ref), None)
            if copy is not None:
                copy(0).wait()

    def need_part(self, ref, i):
        if id(ref) in self.ins:
            self.ins[id(ref)](i).wait()

    def ready(self, *refs):
        for ref in refs:
            copy = self.outs.get(id(ref))
            if copy is not None:
                copy.start()
                self.sent.append(copy)

    def send(self, local, remote):
        copy = pltpu.make_async_copy(local, remote, self.sems[id(remote)])
        copy.start()
        self.sent.append(copy)


def part_copy(remote, local, sems, first, parts):
    size = local.shape[0] // parts

    def copy(i):
        rows = pl.ds(i * size, size)
        return pltpu.make_async_copy(remote.at[rows], local.at[rows], sems.at[first + i])

    return copy


def call(kernel, outs, scratch, args, scalars, name, limit=24):
    info = list(args) + list(outs)
    split = len(args)
    values = [x.value if isinstance(x, Far) else x for x in info]
    far = [isinstance(x, Far) for x in info]
    raw = [isinstance(x, Raw) for x in info]
    buffers, sem_at, count = [], {}, 0
    for i, value in enumerate(values):
        if far[i]:
            sem_at[i] = count
            count += info[i].parts
            if not raw[i]:
                buffers.append(pltpu.VMEM(value.shape, value.dtype) if i < split else pltpu.VMEM(value, F32))

    def whole(*refs):
        sems = refs[-1]
        refs = list(refs[:-1])
        spare = iter(refs[len(info) : len(info) + len(buffers)])
        rest = refs[len(info) + len(buffers) :]
        copies = Copies()
        for i in sem_at:
            first = sem_at[i]
            if raw[i]:
                copies.sems[id(refs[i])] = sems.at[first]
                continue
            remote, local = refs[i], next(spare)
            refs[i] = local
            if i < split:
                copies.ins[id(local)] = part_copy(remote, local, sems, first, info[i].parts)
                for j in range(info[i].parts):
                    copies.ins[id(local)](j).start()
            else:
                copies.outs[id(local)] = pltpu.make_async_copy(local, remote, sems.at[first])
        kernel(copies, *refs[: len(info)], *rest)
        for copy in copies.sent:
            copy.wait()

    far_spec = pl.BlockSpec(memory_space=pltpu.HBM)
    specs = [SM if i < scalars else (far_spec if far[i] else VM) for i in range(len(info))]
    operands = [
        pltpu.with_memory_space_constraint(x, pltpu.HBM) if is_far else x for x, is_far in zip(values[:split], far)
    ]
    return pl.pallas_call(
        whole,
        out_shape=tuple(
            pltpu.HBM(x, F32) if is_far else jax.ShapeDtypeStruct(x, F32) for x, is_far in zip(values[split:], far[split:])
        ),
        in_specs=specs[:split],
        out_specs=tuple(specs[split:]),
        scratch_shapes=buffers
        + [x if x is SPOTS else pltpu.VMEM(x, F32) for x in scratch]
        + [pltpu.SemaphoreType.DMA((max(count, 1),))],
        compiler_params=pltpu.CompilerParams(vmem_limit_bytes=limit * 1024 * 1024),
        name=name,
    )(*operands)


def length(axes):
    return functools.reduce(lambda a, b: a * b, [lax.axis_size(axis) for axis in axes])


def pairs_first(count):
    return [(i, i ^ 1) for i in range(count)]


def pairs_second(count):
    pairs = [(i, i + 1) for i in range(1, count - 1, 2)]
    return pairs + [(j, i) for i, j in pairs]


def exchange(first, second, axes):
    count = length(axes)
    return lax.ppermute(first, axes, pairs_first(count)), lax.ppermute(second, axes, pairs_second(count))


def swap(value, axes):
    count = length(axes)
    return lax.ppermute(value, axes, [(i, count - 1 - i) for i in range(count)])


def share_over_x(share):
    near = swap(share, ("xl",))
    far = swap(share, ("xh",))
    cross = swap(share, ("xh", "xl"))
    at = lax.broadcasted_iota(jnp.int32, share.shape, 0)
    added = (share + near) + (far + cross)
    largest = jnp.maximum(jnp.maximum(share, near), jnp.maximum(far, cross))
    return jnp.where(at < DATA, added, largest)


def body(object_field, probe_modes, scan_offsets, measured):
    n = probe_modes.shape[-1]
    modes = probe_modes.shape[1]
    half = n // 2
    tile = object_field.shape[1]
    extent = tile + n
    blocks = extent // n
    positions = scan_offsets.shape[2]
    offsets = scan_offsets.reshape(positions, 2)
    amplitudes = measured.reshape(positions, n, n)
    tables = dft_pair(n)
    row = lax.axis_index(ROW)
    col = lax.axis_index(COL)
    info = jnp.stack(
        [
            lax.axis_index("core"),
            jnp.where(row == 0, half, 0),
            jnp.where(row == length(ROW) - 1, extent - half, extent),
            jnp.where(col == 0, half, 0),
            jnp.where(col == length(COL) - 1, extent - half, extent),
            row % 2,
            col % 2,
        ]
    ).astype(jnp.int32)

    tag = (offsets + 1).astype(F32).reshape(1, 2 * positions)
    tag_rows = jnp.pad(tag, ((0, 7), (0, n - 2 * positions)))
    edge = (2, half + 8, tile)
    side = (tile + 8, n)
    ends = (n + 8, n)
    row_a, row_b, col_a, col_b = call(
        pack_kernel, [edge, edge, side, side], [], [info, Far(object_field), tag_rows], 1, "pack_edges"
    )
    row_a, row_b = exchange(row_a, row_b, ROW)
    col_a, col_b = exchange(col_a, col_b, COL)
    end_a, end_b = call(corner_kernel, [ends, ends], [], [info, row_a, row_b], 1, "pack_ends")
    halo = [row_a, row_b, col_a, col_b, *exchange(end_a, end_b, COL)]

    cells = (2, blocks, extent, n)
    canvas = (blocks + 2, extent + 2 * n, n)
    lights = (blocks, extent, n)
    grads = (2 * modes + 1, n, n)
    packed = (PARTS * CHUNK, n)
    band = (2, blocks, n, n)
    probes = probe_modes
    tables = [Far(x) for x in tables]
    amplitudes = Far(amplitudes, positions // BATCH)
    for sweep in range(ITERS):
        last = sweep == ITERS - 1
        bands = [(2, blocks, x, n) for x in ((half, half, tile) if last else (n, n, n))]
        outs = [Raw(x) for x in bands] + [packed, packed, Far(cells), Far((n, n))]
        if sweep == 0:
            args = [offsets, info, Far(object_field), tag_rows, *halo, probes, amplitudes, *tables]
            outs = outs + [(16, n)]
            first, second, mid, keep, send, cells_now, bright, tags = call(first_kernel, outs, [cells, grads], args, 2, "first_sweep")
        else:
            held = [Far(x) for x in (cells_now, *sums, light)]
            args = [offsets, info, *held, mine, other, Far(probes), amplitudes, *tables]
            first, second, mid, keep, send, cells_now, bright, probes = call(
                next_kernel, outs + [Far(probes.shape)], [cells, grads], args, 2, "next_sweep"
            )
        if sweep == 0:
            tags = tags[:9, : 2 * positions].astype(jnp.int32)
        received = swap(send, ("core",))
        received, first, second, bright = lax.optimization_barrier((received, first, second, bright))
        parts = lax.all_to_all(keep + received, RING, 0, 0, tiled=True)
        light, peak = call(light_kernel, [Far(lights), (8, n)], [canvas, SPOTS], [tags, Far(bright)], 1, "light")
        row_a, row_b = exchange(first, second, ROW)
        if last:
            parts, row_a, row_b = lax.optimization_barrier((parts, row_a, row_b))
        else:
            parts, row_a = lax.optimization_barrier((parts, row_a))
        share = call(share_kernel, [(CHUNK, n)], [], [parts, peak], 0, "share")[0]
        share = share_over_x(share)
        copies = jnp.broadcast_to(share[None], (PARTS,) + share.shape).reshape(packed)
        light, copies, row_b = lax.optimization_barrier((light, copies, row_b))
        mine = lax.all_to_all(copies, RING, 0, 0, tiled=True)
        if last:
            outs = [Far((2, blocks, tile, n)), Far((tile, n)), Far((tile, n))]
            args = [info] + [Far(x) for x in (mid, row_a, row_b)]
            sums, col_a, col_b = call(fold_inner_kernel, outs, [], args, 1, "fold_inner")
            sums = [sums]
        else:
            side = (2, extent, n)
            outs = [Far(side), Far(side)]
            args = [info] + [Far(x) for x in (first, second, mid, row_a, row_b)]
            col_a, col_b = call(fold_kernel, outs, [], args, 1, "fold_rows")
            sums = [first, second, mid, row_a, row_b]
            args = [tags, Far(bright), Far(light)]
            light = call(more_light_kernel, [Far(lights)], [canvas, SPOTS], args, 1, "more_light")[0]
        col_a, col_b = exchange(col_a, col_b, COL)
        mine, col_a, col_b, light = lax.optimization_barrier((mine, col_a, col_b, light))
        sums += [col_a, col_b]
        other = swap(mine, ("core",))
    held = [Far(x) for x in (cells_now, *sums, light)]
    args = [info, *held, mine, other, Far(probes)]
    return call(last_kernel, [Far(object_field.shape), Far(probes.shape)], [grads], args, 1, "last_update")


def solution(mesh):
    names = tuple(name for name, _ in SPLIT)
    sizes = tuple(size for _, size in SPLIT)
    fine = Mesh(mesh.devices.reshape(sizes), names)
    return jax.shard_map(
        body,
        mesh=fine,
        in_specs=(
            P(None, ROW, COL),
            P(),
            P(ROW, COL, None, None),
            P(ROW, COL, None, None, None),
        ),
        out_specs=(P(None, ROW, COL), P()),
        check_vma=False,
    )
```

```python
import functools

import jax
import jax.numpy as jnp
import numpy as np
from jax import lax
from jax.experimental import pallas as pl
from jax.experimental.pallas import tpu as pltpu
from jax.sharding import Mesh, PartitionSpec as P

ITERS = 2
BATCH = 8
SPLIT = (("y", 4), ("xh", 2), ("core", 2), ("xl", 2), ("z", 8))
ROW = ("y", "xh", "core")
COL = ("xl", "z")
RING = ("y", "z")
PARTS = 32
CHUNK = 24
DATA = 18

VM = pl.BlockSpec(memory_space=pltpu.VMEM)
SM = pl.BlockSpec(memory_space=pltpu.SMEM)
F32 = jnp.float32
SPOTS = pltpu.SMEM((9 * 16 + 4, 2), jnp.int32)


def dft_pair(n):
    index = np.arange(n)
    angle = (index[:, None] * index[None, :] % n) * (2.0 * np.pi / n)
    c = np.cos(angle) / np.sqrt(n)
    s = np.sin(angle) / np.sqrt(n)
    forward = np.block([[c, s], [-s, c]])
    backward = np.block([[c, -s], [s, c]])
    return jnp.asarray(forward, jnp.bfloat16), jnp.asarray(backward, jnp.bfloat16)


def ordered(odd, first, second):
    return jnp.where(odd, first, second), jnp.where(odd, second, first)


def total(values):
    return functools.reduce(jnp.add, values)


def place(canvas, ch, where, lane, value):
    u, k, s = where
    n = value.shape[0]
    rolled = pltpu.roll(value, s, 1)
    canvas[ch, k, pl.ds(u, n), :] += jnp.where(lane >= s, rolled, 0.0)
    canvas[ch, k + 1, pl.ds(u, n), :] += jnp.where(lane >= s, 0.0, rolled)


def sweep_positions(copies, off_ref, probe_ref, meas_ref, fwd_ref, bwd_ref, cells, canvas, grads):
    modes = probe_ref.shape[1]
    n = probe_ref.shape[2]
    grads[...] = jnp.zeros_like(grads)
    lane = lax.broadcasted_iota(jnp.int32, (n, n), 1)

    def window(ch, where):
        u, k, s = where
        left = cells[ch, k, pl.ds(u, n), :]
        right = cells[ch, k + 1, pl.ds(u, n), :]
        return pltpu.roll(jnp.where(lane >= s, left, right), n - s, 1)

    def transform(field, left, right):
        sec = jnp.dot(left, field, preferred_element_type=F32).astype(jnp.bfloat16)
        parts = [slice(m * n, (m + 1) * n) for m in range(modes)]
        rows = [jnp.concatenate([sec[:n, part], sec[n:, part]], 1) for part in parts]
        return jnp.dot(jnp.concatenate(rows, 0), right, preferred_element_type=F32)

    def paired(re_parts, im_parts):
        re_all = jnp.concatenate([x.astype(jnp.bfloat16) for x in re_parts], 1)
        im_all = jnp.concatenate([x.astype(jnp.bfloat16) for x in im_parts], 1)
        return jnp.concatenate([re_all, im_all], 0)

    def split(wave):
        return [(wave[m * n : (m + 1) * n, :n], wave[m * n : (m + 1) * n, n:]) for m in range(modes)]

    def spot(q):
        u = off_ref[q, 0]
        v = off_ref[q, 1]
        return u, v // n, lax.rem(v, n)

    def step(i, carry):
        copies.need_part(meas_ref, i)
        probes = [(probe_ref[0, m], probe_ref[1, m]) for m in range(modes)]
        spots = [spot(i * BATCH + j) for j in range(BATCH)]
        wins = [(window(0, where), window(1, where)) for where in spots]
        exits = []
        for w_re, w_im in wins:
            re_parts = [p_re * w_re - p_im * w_im for p_re, p_im in probes]
            im_parts = [p_re * w_im + p_im * w_re for p_re, p_im in probes]
            exits.append(paired(re_parts, im_parts))
        fars = [split(transform(x, fwd_ref[...], bwd_ref[...])) for x in exits]
        corrected = []
        for j, far in enumerate(fars):
            power = total([re * re + im * im for re, im in far])
            raised = power + 1.0
            root = lax.rsqrt(raised)
            root = root * (1.5 - 0.5 * raised * root * root)
            scale = meas_ref[i * BATCH + j] * root
            corrected.append(paired([re * scale for re, _ in far], [im * scale for _, im in far]))
        backs = [split(transform(x, bwd_ref[...], fwd_ref[...])) for x in corrected]
        for where, back in zip(spots, backs):
            place(canvas, 0, where, lane, total([p[0] * b[0] + p[1] * b[1] for p, b in zip(probes, back)]))
            place(canvas, 1, where, lane, total([p[0] * b[1] - p[1] * b[0] for p, b in zip(probes, back)]))
        for m in range(modes):
            pairs = [(w, back[m]) for w, back in zip(wins, backs)]
            grads[m] += total([w[0] * b[0] + w[1] * b[1] for w, b in pairs])
            grads[modes + m] += total([w[0] * b[1] - w[1] * b[0] for w, b in pairs])
        grads[2 * modes] += total([w[0] * w[0] + w[1] * w[1] for w in wins])
        return carry

    lax.fori_loop(0, meas_ref.shape[0] // BATCH, step, 0)


def pack_half(grads, half, out_ref):
    planes = grads.shape[0]
    out_ref[...] = jnp.zeros_like(out_ref)
    for c in range(planes):
        for t in range(2):
            out_ref[pl.ds(2 * c + t, PARTS, stride=CHUNK), :] = grads[
                c, pl.ds(half * 2 * PARTS + t, PARTS, stride=2), :
            ]


def unpack_half(in_ref, half, grads):
    planes = grads.shape[0]
    for c in range(planes):
        for t in range(2):
            grads[c, pl.ds(half * 2 * PARTS + t, PARTS, stride=2), :] = in_ref[
                pl.ds(2 * c + t, PARTS, stride=CHUNK), :
            ]


def finish(copies, at_ref, canvas, grads, first_ref, second_ref, mid_ref, keep_ref, send_ref):
    band = first_ref.shape[2]
    far = canvas.shape[2] - band
    low = (1 - at_ref[5]) * far
    copies.send(canvas.at[:, :, pl.ds(pl.multiple_of(low, 8), band)], first_ref)
    copies.send(canvas.at[:, :, pl.ds(pl.multiple_of(far - low, 8), band)], second_ref)
    copies.send(canvas.at[:, :, band : band + mid_ref.shape[2]], mid_ref)
    for core in range(2):

        @pl.when(at_ref[0] == core)
        def _():
            pack_half(grads, core, keep_ref)
            pack_half(grads, 1 - core, send_ref)


def brightness(probe_ref):
    return jnp.sum(probe_ref[0] * probe_ref[0] + probe_ref[1] * probe_ref[1], axis=0)


def side_by_side(cells, lane):
    n = lane.shape[1]
    half = n // 2
    size = cells.shape[2]
    left = jnp.where(lane < half, cells[0, :, :n], pltpu.roll(cells[1, :, :n], half, 1))
    right = jnp.where(lane < half, pltpu.roll(cells[0, :, size - n :], half, 1), cells[1, :, size - n :])
    return left, right


def pack_kernel(copies, at_ref, obj_ref, tag_ref, row_a_ref, row_b_ref, col_a_ref, col_b_ref):
    size = obj_ref.shape[1]
    n = col_a_ref.shape[1]
    half = n // 2
    copies.need(obj_ref)
    row_a_ref[:, :half], row_b_ref[:, :half] = ordered(at_ref[5] == 1, obj_ref[:, :half], obj_ref[:, size - half :])
    for ref in (row_a_ref, row_b_ref):
        ref[:, half:] = jnp.zeros((2, 8, size), F32)
        ref[0, half:, :n] = tag_ref[...]
    lane = lax.broadcasted_iota(jnp.int32, (size, n), 1)
    left, right = side_by_side(obj_ref[...], lane)
    col_a_ref[:size], col_b_ref[:size] = ordered(at_ref[6] == 1, left, right)
    col_a_ref[size:] = tag_ref[...]
    col_b_ref[size:] = tag_ref[...]


def corner_kernel(copies, at_ref, row_a_ref, row_b_ref, end_a_ref, end_b_ref):
    n = end_a_ref.shape[1]
    half = n // 2
    lane = lax.broadcasted_iota(jnp.int32, (half, n), 1)
    rows = ordered(at_ref[5] == 1, row_a_ref[...], row_b_ref[...])
    for j, strip in enumerate(rows):
        left, right = side_by_side(strip[:, :half], lane)
        part = slice(j * half, (j + 1) * half)
        end_a_ref[part], end_b_ref[part] = ordered(at_ref[6] == 1, left, right)
    for ref in (end_a_ref, end_b_ref):
        ref[n:] = jnp.zeros((8, n), F32)
        for j, strip in enumerate(rows):
            ref[n + j : n + j + 1] = strip[0, half : half + 1, :n]


def first_kernel(
    copies, off_ref, at_ref, obj_ref, tag_ref,
    row_a_ref, row_b_ref, col_a_ref, col_b_ref, end_a_ref, end_b_ref,
    probe_ref, meas_ref, fwd_ref, bwd_ref,
    first_ref, second_ref, mid_ref, keep_ref, send_ref, cells, bright_ref, tags_ref, canvas, grads,
):
    n = probe_ref.shape[2]
    half = n // 2
    size = obj_ref.shape[1]
    odd_row = at_ref[5] == 1
    odd_col = at_ref[6] == 1
    canvas[...] = jnp.zeros_like(canvas)
    bright_ref[...] = brightness(probe_ref)
    copies.ready(bright_ref)
    upper, lower = ordered(odd_row, row_a_ref[...], row_b_ref[...])
    before, after = ordered(odd_col, col_a_ref[...], col_b_ref[...])
    ends = ordered(odd_col, end_a_ref[...], end_b_ref[...])
    over = [x[:half] for x in ends]
    under = [x[half:n] for x in ends]
    tags_ref[...] = jnp.zeros_like(tags_ref)
    tags_ref[:9] = jnp.concatenate(
        [
            ends[0][n : n + 1], before[size : size + 1], ends[0][n + 1 : n + 2],
            upper[0, half : half + 1, :n], tag_ref[:1], lower[0, half : half + 1, :n],
            ends[1][n : n + 1], after[size : size + 1], ends[1][n + 1 : n + 2],
        ],
        0,
    )
    copies.need(obj_ref)
    bands = (
        (0, half, upper[:, :half], over[0], over[1]),
        (half, size, obj_ref[...], before[:size], after[:size]),
        (half + size, half, lower[:, :half], under[0], under[1]),
    )
    for start, count, centre, left, right in bands:
        rows = slice(start, start + count)
        lane = lax.broadcasted_iota(jnp.int32, (count, n), 1)
        strips = [(left, pltpu.roll(right, half, 1)), (pltpu.roll(left, half, 1), right)]
        for ch in range(2):
            inner = [pltpu.roll(centre[ch, :, k * n : (k + 1) * n], half, 1) for k in range(2)]
            row = [strips[ch][0], *inner, strips[ch][1]]
            for k in range(3):
                cells[ch, k, rows] = jnp.where(lane < half, row[k], row[k + 1])
    copies.ready(cells)
    copies.need(fwd_ref, bwd_ref)
    sweep_positions(copies, off_ref, probe_ref, meas_ref, fwd_ref, bwd_ref, cells, canvas, grads)
    finish(copies, at_ref, canvas, grads, first_ref, second_ref, mid_ref, keep_ref, send_ref)


def light_peak(mine_ref, other_ref):
    best = [jnp.max(ref[pl.ds(DATA, PARTS, stride=CHUNK), :]) for ref in (mine_ref, other_ref)]
    return jnp.maximum(best[0], best[1])


def update_probes(at_ref, mine_ref, other_ref, probe_ref, grads, new_probe_ref):
    modes = probe_ref.shape[1]
    for core in range(2):

        @pl.when(at_ref[0] == core)
        def _():
            unpack_half(mine_ref, core, grads)
            unpack_half(other_ref, 1 - core, grads)

    density = grads[2 * modes]
    scale = 1.0 / (density + 0.1 * jnp.max(density))
    for part in range(2):
        for m in range(modes):
            old = probe_ref[part, m]
            new_probe_ref[part, m] = old + (grads[part * modes + m] - old * density) * scale


def updated(old, sums, light, peak):
    scale = 1.0 / (light + 0.1 * peak)
    return [old[ch] + (sums[ch] - old[ch] * light) * scale for ch in range(2)]


def next_kernel(
    copies, off_ref, at_ref, obj_ref, own_a_ref, own_b_ref, mid_ref, row_a_ref, row_b_ref, col_a_ref, col_b_ref, light_ref,
    mine_ref, other_ref, probe_ref, meas_ref, fwd_ref, bwd_ref,
    first_ref, second_ref, new_mid_ref, keep_ref, send_ref, new_obj_ref, bright_ref, new_probe_ref,
    canvas, grads,
):
    n = probe_ref.shape[2]
    blocks = obj_ref.shape[1]
    canvas[...] = jnp.zeros_like(canvas)
    peak = light_peak(mine_ref, other_ref)
    copies.need(probe_ref)
    update_probes(at_ref, mine_ref, other_ref, probe_ref, grads, new_probe_ref)
    copies.ready(new_probe_ref)
    bright_ref[...] = brightness(new_probe_ref)
    copies.ready(bright_ref)
    copies.need(obj_ref, own_a_ref, own_b_ref, mid_ref, row_a_ref, row_b_ref, col_a_ref, col_b_ref, light_ref)
    for j in range(3):
        rows = slice(j * n, (j + 1) * n)
        row = lax.broadcasted_iota(jnp.int32, (n, n), 0) + j * n
        row_ok = (row >= at_ref[1]) & (row < at_ref[2])
        for k in range(blocks):
            col = lax.broadcasted_iota(jnp.int32, (n, n), 1) + k * n
            inside = row_ok & (col >= at_ref[3]) & (col < at_ref[4])
            if j == 1:
                sums = mid_ref[:, k]
            else:
                ends = ordered(
                    at_ref[5] == 1, own_a_ref[:, k] + row_a_ref[:, k], own_b_ref[:, k] + row_b_ref[:, k]
                )
                sums = ends[j > 0]
            if k in (0, blocks - 1):
                sides = ordered(at_ref[6] == 1, col_a_ref[:, rows], col_b_ref[:, rows])
                sums = sums + sides[k > 0]
            new = updated(obj_ref[:, k, rows], sums, light_ref[k, rows], peak)
            for ch in range(2):
                new_obj_ref[ch, k, rows] = jnp.where(inside, new[ch], 0.0)
    copies.ready(new_obj_ref)
    copies.need(fwd_ref, bwd_ref)
    sweep_positions(copies, off_ref, new_probe_ref, meas_ref, fwd_ref, bwd_ref, new_obj_ref, canvas, grads)
    finish(copies, at_ref, canvas, grads, first_ref, second_ref, new_mid_ref, keep_ref, send_ref)


def last_kernel(
    copies, at_ref, obj_ref, sums_ref, col_a_ref, col_b_ref, light_ref, mine_ref, other_ref, probe_ref,
    out_ref, new_probe_ref, grads,
):
    n = probe_ref.shape[2]
    half = n // 2
    blocks = obj_ref.shape[1]
    tile = out_ref.shape[1]
    inner = slice(half, half + tile)
    copies.need(probe_ref)
    update_probes(at_ref, mine_ref, other_ref, probe_ref, grads, new_probe_ref)
    copies.ready(new_probe_ref)
    copies.need(obj_ref, sums_ref, col_a_ref, col_b_ref, light_ref)
    left, right = ordered(at_ref[6] == 1, col_a_ref[...], col_b_ref[...])
    peak = light_peak(mine_ref, other_ref)
    lane = lax.broadcasted_iota(jnp.int32, (tile, n), 1)
    rolled = []
    for k in range(blocks):
        sums = [sums_ref[ch, k] for ch in range(2)]
        if k == 0:
            sums[0] = sums[0] + jnp.where(lane < half, 0.0, left)
            sums[1] = sums[1] + jnp.where(lane < half, 0.0, pltpu.roll(left, half, 1))
        elif k == blocks - 1:
            sums[0] = sums[0] + jnp.where(lane < half, right, 0.0)
            sums[1] = sums[1] + jnp.where(lane < half, pltpu.roll(right, half, 1), 0.0)
        new = updated(obj_ref[:, k, inner], sums, light_ref[k, inner], peak)
        rolled.append([pltpu.roll(x, half, 1) for x in new])
    for k in range(blocks - 1):
        for ch in range(2):
            out_ref[ch, :, k * n : (k + 1) * n] = jnp.where(lane < half, rolled[k][ch], rolled[k + 1][ch])
    copies.ready(out_ref)


def fold_kernel(copies, at_ref, first_ref, second_ref, mid_ref, row_a_ref, row_b_ref, col_a_ref, col_b_ref):
    n = col_a_ref.shape[2]
    last = mid_ref.shape[1] - 1
    copies.need(first_ref, row_a_ref, second_ref, row_b_ref, mid_ref)
    sides = []
    for k in (0, last):
        top, low = ordered(
            at_ref[5] == 1, first_ref[:, k] + row_a_ref[:, k], second_ref[:, k] + row_b_ref[:, k]
        )
        sides.append((top, mid_ref[:, k], low))
    for j in range(3):
        rows = slice(j * n, (j + 1) * n)
        col_a_ref[:, rows], col_b_ref[:, rows] = ordered(at_ref[6] == 1, sides[0][j], sides[1][j])
    copies.ready(col_a_ref, col_b_ref)


def fold_inner_kernel(copies, at_ref, mid_ref, row_a_ref, row_b_ref, sums_ref, col_a_ref, col_b_ref):
    n = col_a_ref.shape[1]
    band = row_a_ref.shape[2]
    tile = mid_ref.shape[2]
    last = mid_ref.shape[1] - 1
    copies.need(mid_ref, row_a_ref, row_b_ref)
    upper, lower = ordered(at_ref[5] == 1, row_a_ref[...], row_b_ref[...])
    sums_ref[:, :, :band] = mid_ref[:, :, :band] + upper
    sums_ref[:, :, band : tile - band] = mid_ref[:, :, band : tile - band]
    sums_ref[:, :, tile - band :] = mid_ref[:, :, tile - band :] + lower
    lane = lax.broadcasted_iota(jnp.int32, (tile, n), 1)
    left = jnp.where(lane < band, sums_ref[0, 0], pltpu.roll(sums_ref[1, 0], band, 1))
    right = jnp.where(lane < band, pltpu.roll(sums_ref[1, last], band, 1), sums_ref[0, last])
    col_a_ref[...], col_b_ref[...] = ordered(at_ref[6] == 1, left, right)
    copies.ready(col_a_ref, col_b_ref, sums_ref)


def place_lights(tag_ref, bright_ref, canvas, spots, rim, tile):
    n = bright_ref.shape[1]
    half = n // 2
    group = 4
    lane = lax.broadcasted_iota(jnp.int32, (n, n), 1)
    count = jnp.int32(0)
    for t in range(9):
        if rim and t == 4:
            continue
        down, across = t % 3 - 1, t // 3 - 1

        def gather(p, count):
            u = tag_ref[t, 2 * p]
            v = tag_ref[t, 2 * p + 1]
            held = u > 0
            u = u + (n - 1 + down * tile)
            v = v + (n - 1 + across * tile)
            inner = (u > half) & (u < tile + n + half) & (v > half) & (v < tile + n + half)
            if rim:
                held = held & ~inner & (u > 0) & (u < tile + 2 * n) & (v > 0) & (v < tile + 2 * n)
            else:
                held = held & inner
            spots[count, 0] = u
            spots[count, 1] = v
            return count + held.astype(jnp.int32)

        count = lax.fori_loop(0, tag_ref.shape[1] // 2, gather, count, unroll=16)
    for j in range(group):
        spots[count + j, 0] = 0
        spots[count + j, 1] = 0
    canvas[...] = jnp.zeros_like(canvas)
    value = bright_ref[...]

    def step(i, carry):
        held = []
        for j in range(group):
            u = spots[i * group + j, 0]
            v = spots[i * group + j, 1]
            s = lax.rem(v, n)
            held.append((u, v // n, s, pltpu.roll(value, s, 1)))
        for u, k, s, rolled in held:
            canvas[k, pl.ds(u, n), :] += jnp.where(lane >= s, rolled, 0.0)
            canvas[k + 1, pl.ds(u, n), :] += jnp.where(lane >= s, 0.0, rolled)
        return carry

    lax.fori_loop(0, (count + group - 1) // group, step, 0)


def light_kernel(copies, tag_ref, bright_ref, light_ref, peak_ref, canvas, spots):
    n = bright_ref.shape[1]
    half = n // 2
    blocks, extent = light_ref.shape[:2]
    copies.need(bright_ref)
    place_lights(tag_ref, bright_ref, canvas, spots, False, extent - n)
    light_ref[...] = canvas[1 : 1 + blocks, n : n + extent]
    copies.ready(light_ref)
    lane = lax.broadcasted_iota(jnp.int32, (extent - n, n), 1)
    best = None
    for k in range(blocks):
        mine = light_ref[k, half : extent - half]
        if k == 0:
            mine = jnp.where(lane >= half, mine, 0.0)
        elif k == blocks - 1:
            mine = jnp.where(lane < half, mine, 0.0)
        best = mine if best is None else jnp.maximum(best, mine)
    peak_ref[...] = jnp.full(peak_ref.shape, jnp.max(best), F32)


def more_light_kernel(copies, tag_ref, bright_ref, light_ref, all_ref, canvas, spots):
    n = bright_ref.shape[1]
    blocks, extent = light_ref.shape[:2]
    copies.need(bright_ref)
    place_lights(tag_ref, bright_ref, canvas, spots, True, extent - n)
    copies.need(light_ref)
    all_ref[...] = light_ref[...] + canvas[1 : 1 + blocks, n : n + extent]
    copies.ready(all_ref)


def share_kernel(copies, parts_ref, peak_ref, out_ref):
    share = parts_ref[:CHUNK]
    for s in range(1, PARTS):
        share = share + parts_ref[s * CHUNK : (s + 1) * CHUNK]
    row = lax.broadcasted_iota(jnp.int32, share.shape, 0)
    out_ref[...] = jnp.where(row < DATA, share, peak_ref[:1])


class Far:
    def __init__(self, value, parts=1):
        self.value = value
        self.parts = parts


class Raw(Far):
    pass


class Copies:
    def __init__(self):
        self.ins = {}
        self.outs = {}
        self.sems = {}
        self.sent = []

    def need(self, *refs):
        for ref in refs:
            copy = self.ins.pop(id(ref), None)
            if copy is not None:
                copy(0).wait()

    def need_part(self, ref, i):
        if id(ref) in self.ins:
            self.ins[id(ref)](i).wait()

    def ready(self, *refs):
        for ref in refs:
            copy = self.outs.get(id(ref))
            if copy is not None:
                copy.start()
                self.sent.append(copy)

    def send(self, local, remote):
        copy = pltpu.make_async_copy(local, remote, self.sems[id(remote)])
        copy.start()
        self.sent.append(copy)


def part_copy(remote, local, sems, first, parts):
    size = local.shape[0] // parts

    def copy(i):
        rows = pl.ds(i * size, size)
        return pltpu.make_async_copy(remote.at[rows], local.at[rows], sems.at[first + i])

    return copy


def call(kernel, outs, scratch, args, scalars, name, limit=24):
    info = list(args) + list(outs)
    split = len(args)
    values = [x.value if isinstance(x, Far) else x for x in info]
    far = [isinstance(x, Far) for x in info]
    raw = [isinstance(x, Raw) for x in info]
    buffers, sem_at, count = [], {}, 0
    for i, value in enumerate(values):
        if far[i]:
            sem_at[i] = count
            count += info[i].parts
            if not raw[i]:
                buffers.append(pltpu.VMEM(value.shape, value.dtype) if i < split else pltpu.VMEM(value, F32))

    def whole(*refs):
        sems = refs[-1]
        refs = list(refs[:-1])
        spare = iter(refs[len(info) : len(info) + len(buffers)])
        rest = refs[len(info) + len(buffers) :]
        copies = Copies()
        for i in sem_at:
            first = sem_at[i]
            if raw[i]:
                copies.sems[id(refs[i])] = sems.at[first]
                continue
            remote, local = refs[i], next(spare)
            refs[i] = local
            if i < split:
                copies.ins[id(local)] = part_copy(remote, local, sems, first, info[i].parts)
                for j in range(info[i].parts):
                    copies.ins[id(local)](j).start()
            else:
                copies.outs[id(local)] = pltpu.make_async_copy(local, remote, sems.at[first])
        kernel(copies, *refs[: len(info)], *rest)
        for copy in copies.sent:
            copy.wait()

    far_spec = pl.BlockSpec(memory_space=pltpu.HBM)
    specs = [SM if i < scalars else (far_spec if far[i] else VM) for i in range(len(info))]
    operands = [
        pltpu.with_memory_space_constraint(x, pltpu.HBM) if is_far else x for x, is_far in zip(values[:split], far)
    ]
    return pl.pallas_call(
        whole,
        out_shape=tuple(
            pltpu.HBM(x, F32) if is_far else jax.ShapeDtypeStruct(x, F32) for x, is_far in zip(values[split:], far[split:])
        ),
        in_specs=specs[:split],
        out_specs=tuple(specs[split:]),
        scratch_shapes=buffers
        + [x if x is SPOTS else pltpu.VMEM(x, F32) for x in scratch]
        + [pltpu.SemaphoreType.DMA((max(count, 1),))],
        compiler_params=pltpu.CompilerParams(vmem_limit_bytes=limit * 1024 * 1024),
        name=name,
    )(*operands)


def length(axes):
    return functools.reduce(lambda a, b: a * b, [lax.axis_size(axis) for axis in axes])


def pairs_first(count):
    return [(i, i ^ 1) for i in range(count)]


def pairs_second(count):
    pairs = [(i, i + 1) for i in range(1, count - 1, 2)]
    return pairs + [(j, i) for i, j in pairs]


def exchange(first, second, axes):
    count = length(axes)
    return lax.ppermute(first, axes, pairs_first(count)), lax.ppermute(second, axes, pairs_second(count))


def swap(value, axes):
    count = length(axes)
    return lax.ppermute(value, axes, [(i, count - 1 - i) for i in range(count)])


def share_over_x(share):
    near = swap(share, ("xl",))
    far = swap(share, ("xh",))
    cross = swap(share, ("xh", "xl"))
    at = lax.broadcasted_iota(jnp.int32, share.shape, 0)
    added = (share + near) + (far + cross)
    largest = jnp.maximum(jnp.maximum(share, near), jnp.maximum(far, cross))
    return jnp.where(at < DATA, added, largest)


def body(object_field, probe_modes, scan_offsets, measured):
    n = probe_modes.shape[-1]
    modes = probe_modes.shape[1]
    half = n // 2
    tile = object_field.shape[1]
    extent = tile + n
    blocks = extent // n
    positions = scan_offsets.shape[2]
    offsets = scan_offsets.reshape(positions, 2)
    amplitudes = measured.reshape(positions, n, n)
    tables = dft_pair(n)
    row = lax.axis_index(ROW)
    col = lax.axis_index(COL)
    info = jnp.stack(
        [
            lax.axis_index("core"),
            jnp.where(row == 0, half, 0),
            jnp.where(row == length(ROW) - 1, extent - half, extent),
            jnp.where(col == 0, half, 0),
            jnp.where(col == length(COL) - 1, extent - half, extent),
            row % 2,
            col % 2,
        ]
    ).astype(jnp.int32)

    tag = (offsets + 1).astype(F32).reshape(1, 2 * positions)
    tag_rows = jnp.pad(tag, ((0, 7), (0, n - 2 * positions)))
    edge = (2, half + 8, tile)
    side = (tile + 8, n)
    ends = (n + 8, n)
    row_a, row_b, col_a, col_b = call(
        pack_kernel, [edge, edge, side, side], [], [info, Far(object_field), tag_rows], 1, "pack_edges"
    )
    row_a, row_b = exchange(row_a, row_b, ROW)
    col_a, col_b = exchange(col_a, col_b, COL)
    end_a, end_b = call(corner_kernel, [ends, ends], [], [info, row_a, row_b], 1, "pack_ends")
    halo = [row_a, row_b, col_a, col_b, *exchange(end_a, end_b, COL)]

    cells = (2, blocks, extent, n)
    canvas = (blocks + 2, extent + 2 * n, n)
    lights = (blocks, extent, n)
    grads = (2 * modes + 1, n, n)
    packed = (PARTS * CHUNK, n)
    band = (2, blocks, n, n)
    probes = probe_modes
    tables = [Far(x) for x in tables]
    amplitudes = Far(amplitudes, positions // BATCH)
    for sweep in range(ITERS):
        last = sweep == ITERS - 1
        bands = [(2, blocks, x, n) for x in ((half, half, tile) if last else (n, n, n))]
        outs = [Raw(x) for x in bands] + [packed, packed, Far(cells), Far((n, n))]
        if sweep == 0:
            args = [offsets, info, Far(object_field), tag_rows, *halo, probes, amplitudes, *tables]
            outs = outs + [(16, n)]
            first, second, mid, keep, send, cells_now, bright, tags = call(first_kernel, outs, [cells, grads], args, 2, "first_sweep")
        else:
            held = [Far(x) for x in (cells_now, *sums, light)]
            args = [offsets, info, *held, mine, other, Far(probes), amplitudes, *tables]
            first, second, mid, keep, send, cells_now, bright, probes = call(
                next_kernel, outs + [Far(probes.shape)], [cells, grads], args, 2, "next_sweep"
            )
        if sweep == 0:
            tags = tags[:9, : 2 * positions].astype(jnp.int32)
        received = swap(send, ("core",))
        received, first, second, bright = lax.optimization_barrier((received, first, second, bright))
        parts = lax.all_to_all(keep + received, RING, 0, 0, tiled=True)
        light, peak = call(light_kernel, [Far(lights), (8, n)], [canvas, SPOTS], [tags, Far(bright)], 1, "light")
        row_a, row_b = exchange(first, second, ROW)
        if last:
            parts, row_a, row_b = lax.optimization_barrier((parts, row_a, row_b))
        else:
            parts, row_a = lax.optimization_barrier((parts, row_a))
        share = call(share_kernel, [(CHUNK, n)], [], [parts, peak], 0, "share")[0]
        share = share_over_x(share)
        copies = jnp.broadcast_to(share[None], (PARTS,) + share.shape).reshape(packed)
        light, copies, row_b = lax.optimization_barrier((light, copies, row_b))
        mine = lax.all_to_all(copies, RING, 0, 0, tiled=True)
        if last:
            outs = [Far((2, blocks, tile, n)), Far((tile, n)), Far((tile, n))]
            args = [info] + [Far(x) for x in (mid, row_a, row_b)]
            sums, col_a, col_b = call(fold_inner_kernel, outs, [], args, 1, "fold_inner")
            sums = [sums]
        else:
            side = (2, extent, n)
            outs = [Far(side), Far(side)]
            args = [info] + [Far(x) for x in (first, second, mid, row_a, row_b)]
            col_a, col_b = call(fold_kernel, outs, [], args, 1, "fold_rows")
            sums = [first, second, mid, row_a, row_b]
            light, col_a, col_b = lax.optimization_barrier((light, col_a, col_b))
            args = [tags, Far(bright), Far(light)]
            light = call(more_light_kernel, [Far(lights)], [canvas, SPOTS], args, 1, "more_light")[0]
        col_a, col_b = exchange(col_a, col_b, COL)
        if last:
            mine, col_a, col_b, light = lax.optimization_barrier((mine, col_a, col_b, light))
        else:
            mine, light = lax.optimization_barrier((mine, light))
        sums += [col_a, col_b]
        other = swap(mine, ("core",))
    held = [Far(x) for x in (cells_now, *sums, light)]
    args = [info, *held, mine, other, Far(probes)]
    return call(last_kernel, [Far(object_field.shape), Far(probes.shape)], [grads], args, 1, "last_update")


def solution(mesh):
    names = tuple(name for name, _ in SPLIT)
    sizes = tuple(size for _, size in SPLIT)
    fine = Mesh(mesh.devices.reshape(sizes), names)
    return jax.shard_map(
        body,
        mesh=fine,
        in_specs=(
            P(None, ROW, COL),
            P(),
            P(ROW, COL, None, None),
            P(ROW, COL, None, None, None),
        ),
        out_specs=(P(None, ROW, COL), P()),
        check_vma=False,
    )
```
